512 devices in a mesh: ctx: 32 (over x, y), kvh: 8 (over z_lo, core), grp: 2 (over z_hi).
Axes of the slice: x: 4, y: 8, z: 8 (z_hi: 2, z_lo: 4; z = z_hi * 4 + z_lo), core: 2. Of those that a mesh axis runs over, the one named last changes fastest.
Arguments:
- hidden_in: bfloat16 [2, 32, 8192], P(None, None, ('ctx', 'grp')), may hold values from -16 to 16
- norm_gain: bfloat16 [8192], P(('ctx', 'grp')), may hold values from 0.5 to 1.5
- w_qkv: bfloat16 [8192, 8, 1280], P(('ctx', 'grp'), 'kvh'), may hold values from -0.0625 to 0.0625
- qkv_bias: bfloat16 [8, 1280], P('kvh'), may hold values from -40 to 40
- kv_pool: bfloat16 [2, 2, 8, 16384, 128], P('grp', None, 'kvh', 'ctx'), may hold values from -16 to 16
- suffix_lengths: int32 [32], P('ctx'), may hold values from 1 to 512, 8192 in all
- w_out: bfloat16 [8192, 8192], P('kvh', ('ctx', 'grp')), may hold values from -0.0625 to 0.0625
Outputs:
- attention_out: bfloat16 [2, 32, 8192], P(None, None, ('ctx', 'grp'))
The draws below stay inside these ranges and needn't reach their ends.
Inputs may be any that keep to these rules, and one draw needn't show every extreme that they name: `suffix_lengths`: they sum to 8192, and one of them is 512.
All inputs are finite; a program needn't handle non-finite values. No bound on the sum of `suffix_lengths` on one device may be relied on, other than what follows from the above.
Results may differ from the reference program's by a relative error of at most 0.018.
Values may be sent and summed in bfloat16 or wider, within the bound.
A program may use at most 128 MiB of HBM per device.

```python
import math
import jax
import jax.numpy as jnp
import numpy as np
from jax import lax

D = 8192
H = 64
KVH = 8
HD = 128
G = 8
STEPS = 2
SUF = 512
B = 32
SLOTS = 16384


def shared_layout(key):
    direction = jax.random.normal(jax.random.fold_in(key, 7), (KVH, HD), jnp.float32)
    planted = jax.random.normal(jax.random.fold_in(key, 8), (KVH, HD), jnp.float32)
    head_order = jax.random.permutation(jax.random.fold_in(key, 9), KVH)
    chosen = (head_order < KVH // 4).astype(jnp.float32)
    return (direction, planted, chosen)


def draw_hidden_in(key, part):
    key = jax.random.fold_in(key, 3)
    first_key, second_key, third_key = jax.random.split(key, 3)
    position = jnp.arange(D, dtype=jnp.float32) / D
    column_scale = jnp.exp(jax.random.uniform(second_key, (D,), jnp.float32, math.log(0.3), math.log(3.0)))
    row_scale = jnp.exp(jax.random.uniform(third_key, (STEPS, B, 1), jnp.float32, math.log(0.3), math.log(3.0)))
    ramp_scale = jnp.exp(0.5 * math.log(3.0) * position)
    entries = jax.random.truncated_normal(first_key, -6.0, 6.0, (STEPS, B, D), jnp.float32)
    return jnp.clip(row_scale * entries * column_scale * ramp_scale, -16.0, 16.0).astype(jnp.bfloat16)


def draw_qkv_bias(key, part):
    direction, planted, chosen = shared_layout(key)
    key = jax.random.fold_in(key, 1)
    first_key, second_key, third_key, fourth_key = jax.random.split(key, 4)
    amplitude = jax.random.uniform(first_key, (KVH, G, 1), jnp.float32, 0.7, 1.3)
    strength = jax.random.uniform(fourth_key, (KVH,), jnp.float32, 1.0, 2.0)
    picked_group = jax.random.randint(third_key, (KVH,), 0, G)
    group_match = (jnp.arange(G, dtype=jnp.int32)[None, :] == picked_group[:, None]).astype(jnp.float32)
    aligned_share = chosen[:, None] * group_match * strength[:, None]
    jitter = jax.random.truncated_normal(second_key, -6.0, 6.0, (KVH, G + 2, HD), jnp.float32)
    query_part = amplitude * direction[:, None, :] + aligned_share[:, :, None] * planted[:, None, :] + 0.3 * jitter[:, :G]
    key_part = direction[:, None, :] + 0.3 * jitter[:, G:G + 1]
    value_part = jitter[:, G + 1:]
    joined = jnp.concatenate([query_part, key_part, value_part], axis=1)
    return jnp.clip(joined, -40.0, 40.0).reshape(KVH, (G + 2) * HD).astype(jnp.bfloat16)


def draw_kv_pool(key, part):
    direction, planted, chosen = shared_layout(key)
    key = jax.random.fold_in(key, 2)
    first_key = jax.random.fold_in(key, 0)
    third_key = jax.random.fold_in(key, 2)
    fourth_key = jax.random.fold_in(key, 3)
    pool_shape = (2, 2, KVH, SLOTS, HD)
    gaussian = jax.random.truncated_normal(first_key, -6.0, 6.0, pool_shape, jnp.float32)
    page_mark = (jnp.arange(2) == 1).astype(jnp.float32)[:, None, None, None, None]
    kind_mark = (jnp.arange(2) == 0)[None, :, None, None, None]
    values = jax.random.truncated_normal(third_key, -6.0, 6.0, pool_shape, jnp.float32)
    key_values = 2.5 * gaussian + 0.45 * page_mark * direction[None, None, :, None, :]
    quarter = SLOTS // 4
    offsets = jax.random.randint(fourth_key, (KVH, 4), 0, quarter)
    positions = jnp.arange(4, dtype=jnp.int32)[None, :] * quarter + offsets
    plant_hits = (jnp.arange(SLOTS, dtype=jnp.int32)[None, None, :] == positions[:, :, None]).astype(jnp.float32)
    strengths = jnp.array([16.0, 15.85, 15.7, 15.55], jnp.float32)
    plant_level = jnp.sum(plant_hits * strengths[None, :, None], axis=1)
    planted_keys = plant_level[:, :, None] * jnp.where(planted >= 0.0, 1.0, -1.0)[:, None, :]
    plant_mask = chosen[:, None] * jnp.sum(plant_hits, axis=1) > 0.5
    prompt_keys = jnp.where(plant_mask[:, :, None], planted_keys, key_values[0, 0])
    key_values = key_values.at[0, 0].set(prompt_keys)
    pooled = jnp.where(kind_mark, key_values, values)
    return jnp.clip(pooled, -16.0, 16.0).astype(jnp.bfloat16)


def block_scale(rng, shape, cuts, least, largest):
    gain, own = 1.0, jax.random.fold_in(rng, 6)
    for dim, blocks in cuts:
        draws = jnp.exp(jax.random.uniform(jax.random.fold_in(own, dim), (blocks,), jnp.float32, least / len(cuts), largest / len(cuts)))
        gain = gain * jnp.repeat(draws, shape[dim] // blocks).reshape([-1 if axis == dim else 1 for axis in range(len(shape))])
    return gain


def split_up(count, total, reach, slope):
    loads = [(1 << 20) // math.isqrt(grade ** slope) + 1 for grade in range(2, count + 1)]
    surplus, holding = total - reach - (count - 1), [1] * (count - 1)
    while surplus > 0:
        free = [i for i in range(count - 1) if holding[i] < reach]
        pool, remaining = sum([loads[i] for i in free]), surplus
        for i in free:
            addition = min(reach - holding[i], max(1, remaining * loads[i] // pool), surplus)
            holding[i] = holding[i] + addition
            surplus = surplus - addition
    return np.array([reach] + holding)


def uneven_parts(own_key, number_of, total, bound, slope):
    if number_of == 2:
        one = jax.random.randint(own_key, (), max(1, total - bound), min(bound, total - 1) + 1)
        return jnp.stack([one, total - one])
    lengths = jnp.asarray(split_up(number_of, total, bound, slope), jnp.int32)
    couples = (number_of - 1) // 2
    donor, receiver = lengths[1:1 + 2 * couples:2], lengths[2:2 + 2 * couples:2]
    slack = jnp.minimum(donor - 1, bound - receiver)
    passed = jax.random.randint(jax.random.fold_in(own_key, 1), (couples,), 0, 1 << 20) % (slack + 1)
    lengths = lengths.at[1:1 + 2 * couples:2].set(donor - passed).at[2:2 + 2 * couples:2].set(receiver + passed)
    return lengths[jax.random.permutation(jax.random.fold_in(own_key, 2), number_of)]


def centred(own_key, shape, scale, bound, shards=(), kind=jnp.bfloat16):
    values = jax.random.normal(own_key, shape, jnp.float32) * scale
    if len(shards) > 0:
        values = block_scale(own_key, shape, shards, -0.22, 0.18) * values
    return jnp.clip(values, min=-bound, max=bound).astype(kind)


def setup_inputs(seed: int = 0) -> dict:
    streams_of = jax.random.split(jax.random.key(seed), 8)
    hidden_in = draw_hidden_in(jax.random.fold_in(streams_of[7], 71), 0)
    norm_gain = jnp.clip(1.0 + 0.1 * jax.random.normal(streams_of[1], (D,), jnp.float32), 0.5, 1.5).astype(jnp.bfloat16)
    w_qkv = centred(streams_of[2], (D, KVH, (G + 2) * HD), D ** -0.5, 0.0625, ((0, 64), (1, 8)))
    qkv_bias = draw_qkv_bias(jax.random.fold_in(streams_of[7], 71), 0)
    kv_pool = draw_kv_pool(jax.random.fold_in(streams_of[7], 71), 0)
    suffix_lengths = uneven_parts(streams_of[5], B, B * SUF // 2, SUF, 2).astype(jnp.int32)
    w_out = centred(streams_of[6], (H * HD, D), (H * HD) ** -0.5, 0.0625, ((0, 8), (1, 64)))
    return dict(hidden_in=hidden_in, norm_gain=norm_gain, w_qkv=w_qkv, qkv_bias=qkv_bias, kv_pool=kv_pool, suffix_lengths=suffix_lengths, w_out=w_out)


NORM_EPS = 1e-06
FLOOR_SCORE = -1e+30

def round_half(values):
    return lax.optimization_barrier(values.astype(jnp.bfloat16)).astype(jnp.float32)

def merge_parts(first, second):
    best_score = jnp.maximum(first[0], second[0])
    fade_first = jnp.exp(first[0] - best_score)
    fade_second = jnp.exp(second[0] - best_score)
    return (best_score, first[1] * fade_first + second[1] * fade_second, first[2] * fade_first[..., None] + second[2] * fade_second[..., None])

def prefix_scan(queries, keys, values):
    factor = 1.0 / math.sqrt(HD)
    stride = math.gcd(SLOTS, 4096)
    part_shape = queries.shape[:2]

    def advance(position, carry):
        best_score, weight_sum, summed = carry
        offset = (position * stride).astype(jnp.int32)
        key_block = lax.dynamic_slice_in_dim(keys, offset, stride, 0).astype(jnp.float32)
        value_block = lax.dynamic_slice_in_dim(values, offset, stride, 0).astype(jnp.float32)
        scores = jnp.einsum('qgd,sd->qgs', queries, key_block, precision=lax.Precision.HIGHEST) * factor
        raised = jnp.maximum(best_score, lax.optimization_barrier(jnp.max(scores, axis=-1)))
        fade_out = jnp.exp(best_score - raised)
        weights = round_half(jnp.exp(scores - raised[..., None]))
        weight_sum = weight_sum * fade_out + lax.optimization_barrier(jnp.sum(weights, axis=-1))
        summed = summed * fade_out[..., None] + jnp.einsum('qgs,sd->qgd', weights, value_block, precision=lax.Precision.HIGHEST)
        return (raised, weight_sum, summed)
    start = (jnp.full(part_shape, FLOOR_SCORE, jnp.float32), jnp.zeros(part_shape, jnp.float32), jnp.zeros(queries.shape, jnp.float32))
    return lax.fori_loop(0, SLOTS // stride, advance, start)

def reference(hidden_in, norm_gain, w_qkv, qkv_bias, kv_pool, suffix_lengths, w_out):
    widened = hidden_in.astype(jnp.float32)
    inverse = lax.rsqrt(lax.optimization_barrier(jnp.sum(widened * widened, axis=-1, keepdims=True)) / D + NORM_EPS)
    normed = (widened * inverse * norm_gain.astype(jnp.float32)).astype(jnp.bfloat16)
    flat_rows = normed.reshape(STEPS * B, D).astype(jnp.float32)
    projected = jnp.dot(flat_rows, w_qkv.reshape(D, KVH * (G + 2) * HD).astype(jnp.float32), precision=lax.Precision.HIGHEST) + qkv_bias.reshape(-1).astype(jnp.float32)
    projected = projected.astype(jnp.bfloat16).reshape(STEPS, B, KVH, G + 2, HD)
    live_slots = jnp.arange(SUF, dtype=jnp.int32)[None, :] < suffix_lengths[:, None]
    causal = jnp.arange(STEPS, dtype=jnp.int32)[None, :] <= jnp.arange(STEPS, dtype=jnp.int32)[:, None]
    factor = 1.0 / math.sqrt(HD)

    def one_head(head_index):
        head_block = lax.dynamic_index_in_dim(projected, head_index, 2, keepdims=False).astype(jnp.float32)
        queries = head_block[:, :, :G]
        new_keys = head_block[:, :, G]
        new_values = head_block[:, :, G + 1]
        pool_head = lax.dynamic_index_in_dim(kv_pool, head_index, 2, keepdims=False)
        prompt = prefix_scan(queries.reshape(STEPS * B, G, HD), pool_head[0, 0], pool_head[0, 1])
        prompt = tuple((member.reshape((STEPS, B) + member.shape[1:]) for member in prompt))
        cached_keys = pool_head[1, 0].reshape(B, SUF, HD).astype(jnp.float32)
        cached_values = pool_head[1, 1].reshape(B, SUF, HD).astype(jnp.float32)
        cache_scores = jnp.einsum('tbgd,bsd->tbgs', queries, cached_keys, precision=lax.Precision.HIGHEST) * factor
        fresh_scores = jnp.einsum('tbgd,ubd->tbgu', queries, new_keys, precision=lax.Precision.HIGHEST) * factor
        cache_scores = jnp.where(live_slots[None, :, None, :], cache_scores, FLOOR_SCORE)
        fresh_scores = jnp.where(causal[:, None, None, :], fresh_scores, FLOOR_SCORE)
        best_score = jnp.maximum(lax.optimization_barrier(jnp.max(cache_scores, axis=-1)), lax.optimization_barrier(jnp.max(fresh_scores, axis=-1)))
        cache_weights = round_half(jnp.exp(cache_scores - best_score[..., None]))
        fresh_weights = round_half(jnp.exp(fresh_scores - best_score[..., None]))
        weight_sum = lax.optimization_barrier(jnp.sum(cache_weights, axis=-1)) + lax.optimization_barrier(jnp.sum(fresh_weights, axis=-1))
        summed = jnp.einsum('tbgs,bsd->tbgd', cache_weights, cached_values, precision=lax.Precision.HIGHEST)
        summed = summed + jnp.einsum('tbgu,ubd->tbgd', fresh_weights, new_values, precision=lax.Precision.HIGHEST)
        joined = merge_parts(prompt, (best_score, weight_sum, summed))
        return (joined[2] / joined[1][..., None]).astype(jnp.bfloat16)
    heads_out = lax.map(one_head, jnp.arange(KVH, dtype=jnp.int32))
    attended = jnp.transpose(heads_out, (1, 2, 0, 3, 4)).reshape(STEPS * B, H * HD).astype(jnp.float32)
    result = jnp.dot(attended, w_out.astype(jnp.float32), precision=lax.Precision.HIGHEST)
    return result.astype(jnp.bfloat16).reshape(STEPS, B, D)
```

```python
import functools
import math

import jax
import jax.numpy as jnp
from jax import lax
from jax.experimental import pallas as pl
from jax.experimental.pallas import tpu as pltpu
from jax.sharding import PartitionSpec as P

NORM_EPS = 1e-06
FLOOR_SCORE = -1e30
MESH = pl.DeviceIdType.MESH
NX, NY = 4, 8
HD = 128
F32, BF16 = jnp.float32, jnp.bfloat16


def zigzag(k, middle):
    return middle + (1 - 2 * lax.rem(k, 2)) * ((k + 1) // 2)


def wait_bytes(buffer, sem):
    pltpu.make_async_copy(buffer, buffer, sem).wait()


def total(parts):
    return functools.reduce(jnp.add, parts)


def kernel(
    h_any, gain_any, w_any, bias_any, kv_any, len_ref, wo_any, out_ref,
    h_v, gain_v, w_v, bias_v, kv_v, wo_v,
    part, part_in, sq, sq_in,
    mid, mid_in, newkv_in, sq2, sq2_in,
    query, o_out, o_in, lse_out, lse_in, att, res,
    local_sem, send_sem, recv_sem,
):
    ctx, kvh, grp = lax.axis_index("ctx"), lax.axis_index("kvh"), lax.axis_index("grp")
    x, y = ctx // NY, lax.rem(ctx, NY)
    factor = 1.0 / math.sqrt(HD)

    def send(src, dst, phase, target):
        pltpu.make_async_remote_copy(
            src_ref=src, dst_ref=dst, send_sem=send_sem.at[phase], recv_sem=recv_sem.at[phase],
            device_id=target, device_id_type=MESH,
        ).start()

    loads = [
        pltpu.make_async_copy(src, dst, local_sem.at[i])
        for i, (src, dst) in enumerate(
            ((h_any, h_v), (gain_any, gain_v), (w_any, w_v), (bias_any, bias_v), (kv_any, kv_v.at[3]), (wo_any, wo_v))
        )
    ]
    for load in loads:
        load.start()

    def x_peer(i):
        return lax.rem(x + 1 + i, NX)

    def plane_peer(i):
        return lax.rem(y + zigzag(i // 2, 4), NY), lax.rem(grp + 1 - lax.rem(i, 2), 2)

    def y_peer(i):
        return lax.rem(y + zigzag(i, 4), NY)

    def ctx_peer(i):
        return lax.rem(x + zigzag(lax.rem(i, 4), 2), NX) * NY + lax.rem(y + zigzag(i // 4, 4), NY)

    def kvh_peer(i):
        return lax.rem(kvh + 1 + i, 8)

    barrier = pltpu.get_barrier_semaphore()

    def hello(device):
        pl.semaphore_signal(barrier, inc=1, device_id=device, device_id_type=MESH)

    @pl.loop(0, 31)
    def _(i):
        hello({"ctx": ctx_peer(i)})

    @pl.loop(0, 8)
    def _(i):
        hello({"ctx": x * NY + lax.rem(y + i, NY), "grp": 1 - grp})

    @pl.loop(0, 7)
    def _(i):
        hello({"kvh": kvh_peer(i)})

    loads[0].wait()
    loads[1].wait()
    h = h_v[...].astype(F32)
    h = jnp.concatenate([h[t, 8 * b : 8 * b + 8] for b in range(NX) for t in range(2)], axis=0)
    gain = gain_v[...].astype(F32).reshape(1, HD)
    scaled = (h * gain).astype(BF16)
    squares = jnp.sum(h * h, axis=1, keepdims=True)
    lane = lax.broadcasted_iota(jnp.int32, (64, HD), 1)
    row = lax.broadcasted_iota(jnp.int32, (64, HD), 0)
    sq[...] = jnp.sum(jnp.where(lane == row, squares, 0.0), axis=0, keepdims=True)
    loads[2].wait()
    for c in range(5):
        prod = jnp.dot(scaled, w_v[:, 256 * c : 256 * c + 256], preferred_element_type=F32).astype(BF16)
        for half in range(2):
            part[:, 2 * c + half] = prod[:, HD * half : HD * half + HD].reshape(NX, 16, HD)

    pl.semaphore_wait(barrier, 46)

    @pl.loop(0, 3)
    def _(i):
        to = x_peer(i)
        send(part.at[to], part_in.at[i], 0, {"ctx": to * NY + y})
        send(sq, sq_in.at[i], 1, {"ctx": to * NY + y})

    @pl.when(grp == 0)
    def _():
        @pl.loop(0, 3)
        def _(i):
            send(kv_any, kv_v.at[i], 2, {"ctx": x_peer(i) * NY + y})

    wait_bytes(part_in, recv_sem.at[0])
    wait_bytes(sq_in, recv_sem.at[1])
    mid[...] = (total([part_in[i].astype(F32) for i in range(3)]) + part[x].astype(F32)).astype(BF16)
    sq2[...] = total([sq_in[i] for i in range(3)]) + sq[...]

    @pl.loop(0, 15)
    def _(i):
        to_y, to_grp = plane_peer(i)
        to = {"ctx": x * NY + to_y, "grp": to_grp}
        send(mid.at[to_y], mid_in.at[i], 3, to)
        send(sq2, sq2_in.at[i], 5, to)

        @pl.when(to_grp == 1)
        def _():
            send(mid.at[pl.ds(8, 2)], newkv_in.at[i], 4, to)

    loads[3].wait()
    wait_bytes(sq2_in, recv_sem.at[5])
    lane = lax.broadcasted_iota(jnp.int32, (16, HD), 1)
    row = lax.broadcasted_iota(jnp.int32, (16, HD), 0)
    squares = total([sq2_in[i] for i in range(15)]) + sq2[...]
    squares = jnp.sum(jnp.where(lane == row + 16 * x, squares, 0.0), axis=1, keepdims=True)
    inverse = lax.rsqrt(squares / 8192.0 + NORM_EPS)
    wait_bytes(mid_in, recv_sem.at[3])
    summed = total([mid_in[i].astype(F32) for i in range(15)]) + mid[y].astype(F32)
    bias = bias_v[:, pl.ds(pl.multiple_of(y * HD, HD), HD)].astype(F32)
    query[y] = (summed * inverse + bias).astype(BF16)

    @pl.loop(0, 7)
    def _(i):
        send(query.at[y], query.at[y], 6, {"ctx": x * NY + y_peer(i)})

    loads[4].wait()
    wait_bytes(query.at[pl.ds(0, 7)], recv_sem.at[6])

    def finish(best, weight_sum, out, valid):
        lse = best + jnp.log(weight_sum)
        if valid is not None:
            lse = jnp.where(valid, lse, FLOOR_SCORE)
        o_out[...] = (out / weight_sum).astype(BF16).reshape(8, 16, HD)
        lane = lax.broadcasted_iota(jnp.int32, (HD, HD), 1)
        row = lax.broadcasted_iota(jnp.int32, (HD, HD), 0)
        lse_out[...] = jnp.sum(jnp.where(lane == row, lse, 0.0), axis=0, keepdims=True)

    def scores_of(q, keys):
        return lax.dot_general(q, keys, (((1,), (1,)), ((), ())), preferred_element_type=F32) * factor

    @pl.when(grp == 0)
    def _():
        wait_bytes(kv_v.at[pl.ds(0, 3)], recv_sem.at[2])
        q = query[...].reshape(HD, HD)
        scores = [scores_of(q, kv_v[i, 0]) for i in range(NX)]
        best = functools.reduce(jnp.maximum, [jnp.max(s, axis=1, keepdims=True) for s in scores])
        weights = [jnp.exp(s - best).astype(BF16) for s in scores]
        weight_sum = total([jnp.sum(w.astype(F32), axis=1, keepdims=True) for w in weights])
        out = total([jnp.dot(w, kv_v[i, 1], preferred_element_type=F32) for i, w in enumerate(weights)])
        finish(best, weight_sum, out, None)

    @pl.when(grp == 1)
    def _():
        wait_bytes(newkv_in, recv_sem.at[4])
        fresh = total([newkv_in[i].astype(F32) for i in range(15)]) + mid[8:10].astype(F32)
        new_bias = bias_v[:, 8 * HD :].astype(F32)
        new_keys = (fresh[0] * inverse + new_bias[:, :HD]).astype(BF16)
        new_values = (fresh[1] * inverse + new_bias[:, HD:]).astype(BF16)
        q = query[...].reshape(HD, HD)
        cached = scores_of(q, kv_v[3, 0])
        slot = lax.broadcasted_iota(jnp.int32, cached.shape, 1)
        cached = jnp.where(slot < len_ref[0], cached, FLOOR_SCORE)
        new = scores_of(q, new_keys)
        key_row = lax.broadcasted_iota(jnp.int32, new.shape, 1)
        q_row = lax.broadcasted_iota(jnp.int32, new.shape, 0)
        seen = (lax.rem(key_row, 8) == y) & (key_row // 8 <= lax.rem(q_row // 8, 2))
        new = jnp.where(seen, new, FLOOR_SCORE)
        best = jnp.maximum(jnp.max(cached, axis=1, keepdims=True), jnp.max(new, axis=1, keepdims=True))
        cached = jnp.exp(cached - best).astype(BF16)
        new = jnp.exp(new - best).astype(BF16)
        weight_sum = jnp.sum(cached.astype(F32), axis=1, keepdims=True) + jnp.sum(new.astype(F32), axis=1, keepdims=True)
        out = jnp.dot(cached, kv_v[3, 1], preferred_element_type=F32)
        out = out + jnp.dot(new, new_values, preferred_element_type=F32)
        own = lax.rem(lax.broadcasted_iota(jnp.int32, (HD, 1), 0), 8) == y
        finish(best, weight_sum, out, own)

    @pl.loop(0, 15)
    def _(i):
        to_y, to_grp = plane_peer(i)
        to = {"ctx": x * NY + to_y, "grp": to_grp}
        send(o_out.at[to_y], o_in.at[i], 7, to)
        send(lse_out, lse_in.at[i], 8, to)

    wait_bytes(lse_in, recv_sem.at[8])
    mine = lane == row + 16 * y
    lses = [lse_in[i] for i in range(15)] + [lse_out[...]]
    lses = [jnp.sum(jnp.where(mine, v, 0.0), axis=1, keepdims=True) for v in lses]
    best = functools.reduce(jnp.maximum, lses)
    shares = [jnp.exp(v - best) for v in lses]
    wait_bytes(o_in, recv_sem.at[7])
    outs = [o_in[i].astype(F32) for i in range(15)] + [o_out[y].astype(F32)]
    joined = total([o * s for o, s in zip(outs, shares)]) / total(shares)
    own = y * NX + x
    att[own] = joined.astype(BF16)

    @pl.loop(0, 31)
    def _(i):
        send(att.at[own], att.at[own], 9, {"ctx": ctx_peer(i)})

    loads[5].wait()
    wait_bytes(att.at[pl.ds(0, 31)], recv_sem.at[9])
    projected = total(
        [
            jnp.dot(att[4 * j : 4 * j + 4].reshape(64, HD), wo_v[HD * j : HD * j + HD], preferred_element_type=F32)
            for j in range(8)
        ]
    )
    ordered = [projected[16 * b + 8 * t : 16 * b + 8 * t + 8] for t in range(2) for b in range(NX)]
    res[kvh] = jnp.concatenate(ordered, axis=0).astype(BF16)

    @pl.loop(0, 7)
    def _(i):
        send(res.at[kvh], res.at[kvh], 10, {"kvh": kvh_peer(i)})

    wait_bytes(part_in, send_sem.at[0])
    wait_bytes(sq_in, send_sem.at[1])
    wait_bytes(mid_in, send_sem.at[3])
    wait_bytes(sq2_in, send_sem.at[5])

    @pl.when(grp == 0)
    def _():
        wait_bytes(kv_v.at[pl.ds(0, 3)], send_sem.at[2])
        wait_bytes(newkv_in.at[pl.ds(0, 8)], send_sem.at[4])

    @pl.when(grp == 1)
    def _():
        wait_bytes(newkv_in.at[pl.ds(0, 7)], send_sem.at[4])

    wait_bytes(query.at[pl.ds(0, 7)], send_sem.at[6])
    wait_bytes(o_in, send_sem.at[7])
    wait_bytes(lse_in, send_sem.at[8])
    wait_bytes(att.at[pl.ds(0, 31)], send_sem.at[9])
    wait_bytes(res.at[pl.ds(0, 7)], send_sem.at[10])
    wait_bytes(res.at[pl.ds(0, 7)], recv_sem.at[10])
    out_ref[...] = total([res[k].astype(F32) for k in range(8)]).astype(BF16).reshape(2, 32, HD)


def local(hidden_in, norm_gain, w_qkv, qkv_bias, kv_pool, suffix_lengths, w_out):
    anywhere = pl.BlockSpec(memory_space=pl.ANY)
    vmem = pltpu.VMEM
    return pl.pallas_call(
        kernel,
        out_shape=jax.ShapeDtypeStruct((2, 32, HD), BF16),
        in_specs=[anywhere] * 5 + [pl.BlockSpec(memory_space=pltpu.SMEM), anywhere],
        out_specs=pl.BlockSpec(memory_space=vmem),
        scratch_shapes=[
            vmem((2, 32, HD), BF16), vmem((HD,), BF16), vmem((HD, 1280), BF16), vmem((1, 1280), BF16),
            vmem((4, 2, 512, HD), BF16), vmem((1024, HD), BF16),
            vmem((4, 10, 16, HD), BF16), vmem((3, 10, 16, HD), BF16), vmem((1, HD), F32), vmem((3, 1, HD), F32),
            vmem((10, 16, HD), BF16), vmem((15, 16, HD), BF16), vmem((15, 2, 16, HD), BF16),
            vmem((1, HD), F32), vmem((15, 1, HD), F32),
            vmem((8, 16, HD), BF16), vmem((8, 16, HD), BF16), vmem((15, 16, HD), BF16),
            vmem((1, HD), F32), vmem((15, 1, HD), F32), vmem((32, 16, HD), BF16), vmem((8, 64, HD), BF16),
            pltpu.SemaphoreType.DMA((6,)), pltpu.SemaphoreType.DMA((11,)), pltpu.SemaphoreType.DMA((11,)),
        ],
        compiler_params=pltpu.CompilerParams(
            collective_id=0, has_side_effects=True, vmem_limit_bytes=60 << 20
        ),
        name="attention_block",
    )(
        hidden_in, norm_gain, w_qkv.reshape(HD, 1280), qkv_bias, kv_pool.reshape(2, 512, HD),
        suffix_lengths, w_out,
    )


def solution(mesh):
    placed = (
        P(None, None, ("ctx", "grp")),
        P(("ctx", "grp")),
        P(("ctx", "grp"), "kvh", None),
        P("kvh", None),
        P("grp", None, "kvh", "ctx", None),
        P("ctx"),
        P("kvh", ("ctx", "grp")),
    )
    return jax.shard_map(
        local, mesh=mesh, in_specs=placed, out_specs=P(None, None, ("ctx", "grp")), check_vma=False
    )
```

```python
import functools
import math

import jax
import jax.numpy as jnp
from jax import lax
from jax.experimental import pallas as pl
from jax.experimental.pallas import tpu as pltpu
from jax.sharding import PartitionSpec as P

NORM_EPS = 1e-06
FLOOR_SCORE = -1e30
MESH = pl.DeviceIdType.MESH
NX, NY = 4, 8
HD = 128
F32, BF16 = jnp.float32, jnp.bfloat16


def zigzag(k, middle):
    return middle + (1 - 2 * lax.rem(k, 2)) * ((k + 1) // 2)


def wait_bytes(buffer, sem):
    pltpu.make_async_copy(buffer, buffer, sem).wait()


def total(parts):
    return functools.reduce(jnp.add, parts)


def kernel(
    h_any, gain_any, w_any, bias_any, kv_any, len_ref, wo_any, out_ref,
    h_v, gain_v, w_v, bias_v, kv_v, wo_v, head_bias,
    part, part_in, sq, sq_in, direct_in, direct_sq_in,
    mid, mid_in, rows, pairs, pairs_in, sq2, sq2_in,
    query, o_out, o_in, lse_out, lse_in, suf_out, suf_in, att, res,
    local_sem, send_sem, recv_sem, hello_sem,
):
    ctx, kvh, grp = lax.axis_index("ctx"), lax.axis_index("kvh"), lax.axis_index("grp")
    x, y = ctx // NY, lax.rem(ctx, NY)
    factor = 1.0 / math.sqrt(HD)

    def send(src, dst, phase, target):
        pltpu.make_async_remote_copy(
            src_ref=src, dst_ref=dst, send_sem=send_sem.at[phase], recv_sem=recv_sem.at[phase],
            device_id=target, device_id_type=MESH,
        ).start()

    loads = [
        pltpu.make_async_copy(src, dst, local_sem.at[i])
        for i, (src, dst) in enumerate(
            ((h_any, h_v), (gain_any, gain_v), (w_any, w_v), (bias_any, bias_v), (kv_any, kv_v.at[3]), (wo_any, wo_v))
        )
    ]
    for load in loads:
        load.start()

    def x_peer(i):
        return lax.rem(x + zigzag(i, 2), NX) * NY + y

    def y_peer(i):
        return lax.rem(y + zigzag(i, 4), NY)

    def column(to_y):
        return x * NY + to_y

    def plane_peer(i):
        return lax.rem(x + zigzag(lax.rem(i, 4), 2), NX), lax.rem(y + zigzag(i // 4, 4), NY)

    def kvh_peer(i):
        return lax.rem(kvh + 1 + i, 8)

    barrier = pltpu.get_barrier_semaphore()

    def greet(device):
        pl.semaphore_signal(barrier, inc=1, device_id=device, device_id_type=MESH)

    @pl.loop(0, 3)
    def _(i):
        greet({"ctx": x_peer(i)})

    @pl.loop(0, 7)
    def _(i):
        greet({"kvh": kvh_peer(i)})

    @pl.loop(0, 7)
    def _(i):
        greet({"ctx": column(y_peer(i))})

    @pl.when(grp == 0)
    def _():
        @pl.loop(0, 32)
        def _(i):
            greet({"ctx": i, "grp": 1})

    loads[0].wait()
    loads[1].wait()
    h = h_v[...].astype(F32)
    h = jnp.concatenate([h[t, 8 * b : 8 * b + 8] for b in range(NX) for t in range(2)], axis=0)
    gain = gain_v[...].astype(F32).reshape(1, HD)
    scaled = (h * gain).astype(BF16)
    squares = jnp.sum(h * h, axis=1, keepdims=True)
    lane = lax.broadcasted_iota(jnp.int32, (64, HD), 1)
    row = lax.broadcasted_iota(jnp.int32, (64, HD), 0)
    sq[...] = jnp.sum(jnp.where(lane == row, squares, 0.0), axis=0, keepdims=True)
    loads[2].wait()
    for c in range(5):
        prod = jnp.dot(scaled, w_v[:, 256 * c : 256 * c + 256], preferred_element_type=F32).astype(BF16)
        for half in range(2):
            part[:, 2 * c + half] = prod[:, HD * half : HD * half + HD].reshape(NX, 16, HD)

    @pl.when(grp == 0)
    def _():
        pl.semaphore_wait(barrier, 17)

    @pl.when(grp == 1)
    def _():
        pl.semaphore_wait(barrier, 49)

        @pl.loop(0, 8)
        def _(i):
            there = {"ctx": column(y_peer(i)), "grp": 0}
            pl.semaphore_signal(hello_sem, inc=1, device_id=there, device_id_type=MESH)

        @pl.loop(0, 32)
        def _(i):
            to_x, to_y = plane_peer(i)
            to = {"ctx": to_x * NY + to_y, "grp": 0}
            send(part.at[to_x, to_y], direct_in.at[ctx], 6, to)
            send(sq, direct_sq_in.at[ctx], 7, to)

    @pl.loop(0, 3)
    def _(i):
        to = x_peer(i)
        send(part.at[to // NY], part_in.at[i], 0, {"ctx": to})
        send(sq, sq_in.at[i], 1, {"ctx": to})

    @pl.when(grp == 0)
    def _():
        @pl.loop(0, 3)
        def _(i):
            send(kv_any, kv_v.at[i], 2, {"ctx": x_peer(i)})

    rows[...] = jnp.zeros_like(rows)
    loads[3].wait()
    for j in range(8):
        head_bias[j : j + 1] = bias_v[:, HD * j : HD * j + HD].astype(F32)
    head_bias[8:16] = head_bias[0:8]
    head_bias[16:24] = jnp.broadcast_to(bias_v[:, 8 * HD : 9 * HD].astype(F32), (8, HD))
    head_bias[24:32] = jnp.broadcast_to(bias_v[:, 9 * HD :].astype(F32), (8, HD))
    wait_bytes(sq_in, recv_sem.at[1])
    sq2[...] = total([sq_in[i] for i in range(3)]) + sq[...]
    wait_bytes(part_in, recv_sem.at[0])
    line = total([part_in[i].astype(F32) for i in range(3)]) + part[x].astype(F32)

    @pl.when(grp == 0)
    def _():
        mid[...] = line.astype(BF16)

        @pl.loop(0, 7)
        def _(i):
            to_y = y_peer(i)
            send(mid.at[to_y], mid_in.at[i], 3, {"ctx": column(to_y)})
            send(sq2, sq2_in.at[i], 5, {"ctx": column(to_y)})

    rows[0:144] = line[0:9].reshape(144, HD)
    rows[192:208] = line[9]
    for b in range(8):
        pieces = [rows[pl.ds(b + first, 8, stride=step)] for first, step in ((0, 16), (8, 16), (128, 8), (192, 8))]
        pairs[b] = jnp.concatenate(pieces, axis=0).astype(BF16)

    @pl.when(grp == 0)
    def _():
        pl.semaphore_wait(hello_sem, 8)

        @pl.loop(0, 8)
        def _(i):
            to_y = y_peer(i)
            to = {"ctx": column(to_y), "grp": 1}
            send(pairs.at[to_y], pairs_in.at[7 + i], 4, to)
            send(sq2, sq2_in.at[7 + i], 5, to)

        lane = lax.broadcasted_iota(jnp.int32, (16, HD), 1)
        row = lax.broadcasted_iota(jnp.int32, (16, HD), 0)
        wait_bytes(sq2_in.at[pl.ds(0, 7)], recv_sem.at[5])
        wait_bytes(mid_in, recv_sem.at[3])
        squares = total([sq2_in[i] for i in range(7)]) + sq2[...]
        summed = total([mid_in[i].astype(F32) for i in range(7)]) + mid[y].astype(F32)
        bias = bias_v[:, pl.ds(pl.multiple_of(y * HD, HD), HD)].astype(F32)
        wait_bytes(direct_sq_in, recv_sem.at[7])
        squares = total([direct_sq_in[i] for i in range(32)]) + squares
        squares = jnp.sum(jnp.where(lane == row + 16 * x, squares, 0.0), axis=1, keepdims=True)
        inverse = lax.rsqrt(squares / 8192.0 + NORM_EPS)
        wait_bytes(direct_in, recv_sem.at[6])
        summed = total([direct_in[i].astype(F32) for i in range(32)]) + summed
        query[y] = (summed * inverse + bias).astype(BF16)

        @pl.loop(0, 7)
        def _(i):
            send(query.at[y], query.at[y], 8, {"ctx": column(y_peer(i))})

    @pl.when(grp == 1)
    def _():
        @pl.loop(0, 7)
        def _(i):
            to_y = y_peer(i)
            send(pairs.at[to_y], pairs_in.at[i], 4, {"ctx": column(to_y)})
            send(sq2, sq2_in.at[i], 5, {"ctx": column(to_y)})

    def scores_of(q, keys):
        return lax.dot_general(q, keys, (((1,), (1,)), ((), ())), preferred_element_type=F32) * factor

    @pl.when(grp == 0)
    def _():
        loads[4].wait()
        wait_bytes(kv_v.at[pl.ds(0, 3)], recv_sem.at[2])
        wait_bytes(query.at[pl.ds(0, 7)], recv_sem.at[8])
        q = query[...].reshape(HD, HD)
        scores = [scores_of(q, kv_v[i, 0]) for i in range(NX)]
        best = functools.reduce(jnp.maximum, [jnp.max(s, axis=1, keepdims=True) for s in scores])
        weights = [jnp.exp(s - best).astype(BF16) for s in scores]
        weight_sum = total([jnp.sum(w.astype(F32), axis=1, keepdims=True) for w in weights])
        out = total([jnp.dot(w, kv_v[i, 1], preferred_element_type=F32) for i, w in enumerate(weights)])
        o_out[...] = (out / weight_sum).astype(BF16).reshape(8, 16, HD)
        lse = best + jnp.log(weight_sum)
        lane = lax.broadcasted_iota(jnp.int32, (HD, HD), 1)
        row = lax.broadcasted_iota(jnp.int32, (HD, HD), 0)
        lse_out[...] = jnp.sum(jnp.where(lane == row, lse, 0.0), axis=0, keepdims=True)

        @pl.loop(0, 15)
        def _(i):
            to_y, to_grp = y_peer(i // 2), 1 - lax.rem(i, 2)
            to = {"ctx": column(to_y), "grp": to_grp}
            send(o_out.at[to_y], o_in.at[y], 9, to)
            send(lse_out, lse_in.at[y], 10, to)

        o_in[y] = o_out[y]
        lse_in[y] = lse_out[...]

    @pl.when(grp == 1)
    def _():
        lane = lax.broadcasted_iota(jnp.int32, (32, HD), 1)
        row = lax.broadcasted_iota(jnp.int32, (32, HD), 0)
        step = jnp.where(row < 16, row // 8, lax.rem(row, 2))
        wait_bytes(sq2_in, recv_sem.at[5])
        squares = total([sq2_in[i] for i in range(15)]) + sq2[...]
        squares = jnp.sum(jnp.where(lane == 16 * x + 8 * step + y, squares, 0.0), axis=1, keepdims=True)
        inverse = lax.rsqrt(squares / 8192.0 + NORM_EPS)
        wait_bytes(pairs_in, recv_sem.at[4])
        summed = total([pairs_in[i].astype(F32) for i in range(15)]) + pairs[y].astype(F32)
        summed = (summed * inverse + head_bias[...]).astype(BF16)
        loads[4].wait()
        q = summed[0:16]
        fresh = summed[16:32]
        cached = scores_of(q, kv_v[3, 0])
        slot = lax.broadcasted_iota(jnp.int32, cached.shape, 1)
        cached = jnp.where(slot < len_ref[0], cached, FLOOR_SCORE)
        new = scores_of(q, fresh)
        key_step = lax.broadcasted_iota(jnp.int32, new.shape, 1)
        q_step = lax.broadcasted_iota(jnp.int32, new.shape, 0) // 8
        new = jnp.where(key_step <= q_step, new, FLOOR_SCORE)
        best = jnp.maximum(jnp.max(cached, axis=1, keepdims=True), jnp.max(new, axis=1, keepdims=True))
        cached = jnp.exp(cached - best).astype(BF16)
        new = jnp.exp(new - best).astype(BF16)
        weight_sum = jnp.sum(cached.astype(F32), axis=1, keepdims=True) + jnp.sum(new.astype(F32), axis=1, keepdims=True)
        out = jnp.dot(cached, kv_v[3, 1], preferred_element_type=F32)
        values = jnp.concatenate([summed[24:32].astype(F32), jnp.zeros((8, HD), F32)], axis=0).astype(BF16)
        out = out + jnp.dot(new, values, preferred_element_type=F32)
        out = out / weight_sum
        lse = jnp.broadcast_to(best + jnp.log(weight_sum), (16, HD))
        for t in range(2):
            suf_out[pl.ds(t, 8, stride=8)] = out[8 * t : 8 * t + 8]
            suf_out[pl.ds(2 + t, 8, stride=8)] = lse[8 * t : 8 * t + 8]
        zero = jnp.zeros((8, HD), F32)
        for t in range(4, 8):
            suf_out[pl.ds(t, 8, stride=8)] = zero

        @pl.loop(0, 15)
        def _(i):
            to_y, to_grp = y_peer(i // 2), lax.rem(i, 2)
            to = {"ctx": column(to_y), "grp": to_grp}
            send(suf_out.at[pl.ds(pl.multiple_of(8 * to_y, 8), 8)], suf_in.at[pl.ds(pl.multiple_of(8 * y, 8), 8)], 11, to)

        mine = pl.ds(pl.multiple_of(8 * y, 8), 8)
        suf_in[mine] = suf_out[mine]

    @pl.when(grp == 0)
    def _():
        wait_bytes(lse_in.at[pl.ds(0, 7)], recv_sem.at[10])
        wait_bytes(suf_in, recv_sem.at[11])
        wait_bytes(o_in.at[pl.ds(0, 7)], recv_sem.at[9])

    @pl.when(grp == 1)
    def _():
        wait_bytes(lse_in, recv_sem.at[10])
        wait_bytes(suf_in.at[pl.ds(0, 56)], recv_sem.at[11])
        wait_bytes(o_in, recv_sem.at[9])

    lane = lax.broadcasted_iota(jnp.int32, (16, HD), 1)
    row = lax.broadcasted_iota(jnp.int32, (16, HD), 0)
    mine = lane == row + 16 * y
    lses = [jnp.sum(jnp.where(mine, lse_in[i], 0.0), axis=1, keepdims=True) for i in range(8)]
    lses.append(jnp.concatenate([suf_in[pl.ds(2 + t, 8, stride=8)] for t in range(2)], axis=0)[:, 0:1])
    best = functools.reduce(jnp.maximum, lses)
    shares = [jnp.exp(v - best) for v in lses]
    outs = [o_in[i].astype(F32) for i in range(8)]
    outs.append(jnp.concatenate([suf_in[pl.ds(t, 8, stride=8)] for t in range(2)], axis=0))
    joined = total([o * s for o, s in zip(outs, shares)]) / total(shares)
    own = y * NX + x
    att[own] = joined.astype(BF16)

    @pl.loop(0, 31)
    def _(i):
        to_x, to_y = plane_peer(i)
        send(att.at[own], att.at[own], 12, {"ctx": to_x * NY + to_y})

    loads[5].wait()
    wait_bytes(att.at[pl.ds(0, 31)], recv_sem.at[12])
    projected = total(
        [
            jnp.dot(att[4 * j : 4 * j + 4].reshape(64, HD), wo_v[HD * j : HD * j + HD], preferred_element_type=F32)
            for j in range(8)
        ]
    )
    ordered = [projected[16 * b + 8 * t : 16 * b + 8 * t + 8] for t in range(2) for b in range(NX)]
    res[kvh] = jnp.concatenate(ordered, axis=0).astype(BF16)

    @pl.loop(0, 7)
    def _(i):
        send(res.at[kvh], res.at[kvh], 13, {"kvh": kvh_peer(i)})


    @pl.when(grp == 1)
    def _():
        wait_bytes(direct_in, send_sem.at[6])
        wait_bytes(direct_sq_in, send_sem.at[7])

    wait_bytes(part_in, send_sem.at[0])
    wait_bytes(sq_in, send_sem.at[1])

    @pl.when(grp == 0)
    def _():
        wait_bytes(kv_v.at[pl.ds(0, 3)], send_sem.at[2])

    @pl.when(grp == 0)
    def _():
        wait_bytes(mid_in, send_sem.at[3])
        wait_bytes(sq2_in, send_sem.at[5])
        wait_bytes(pairs_in.at[pl.ds(0, 8)], send_sem.at[4])
        wait_bytes(query.at[pl.ds(0, 7)], send_sem.at[8])

    @pl.when(grp == 1)
    def _():
        wait_bytes(sq2_in.at[pl.ds(0, 7)], send_sem.at[5])
        wait_bytes(pairs_in.at[pl.ds(0, 7)], send_sem.at[4])

    @pl.when(grp == 0)
    def _():
        wait_bytes(o_in, send_sem.at[9])
        wait_bytes(o_in.at[pl.ds(0, 7)], send_sem.at[9])
        wait_bytes(lse_in, send_sem.at[10])
        wait_bytes(lse_in.at[pl.ds(0, 7)], send_sem.at[10])

    @pl.when(grp == 1)
    def _():
        wait_bytes(suf_in, send_sem.at[11])
        wait_bytes(suf_in.at[pl.ds(0, 56)], send_sem.at[11])

    wait_bytes(att.at[pl.ds(0, 31)], send_sem.at[12])
    wait_bytes(res.at[pl.ds(0, 7)], send_sem.at[13])
    wait_bytes(res.at[pl.ds(0, 7)], recv_sem.at[13])
    out_ref[...] = total([res[k].astype(F32) for k in range(8)]).astype(BF16).reshape(2, 32, HD)


def local(hidden_in, norm_gain, w_qkv, qkv_bias, kv_pool, suffix_lengths, w_out):
    anywhere = pl.BlockSpec(memory_space=pl.ANY)
    vmem = pltpu.VMEM
    return pl.pallas_call(
        kernel,
        out_shape=jax.ShapeDtypeStruct((2, 32, HD), BF16),
        in_specs=[anywhere] * 5 + [pl.BlockSpec(memory_space=pltpu.SMEM), anywhere],
        out_specs=pl.BlockSpec(memory_space=vmem),
        scratch_shapes=[
            vmem((2, 32, HD), BF16), vmem((HD,), BF16), vmem((HD, 1280), BF16), vmem((1, 1280), BF16),
            vmem((4, 2, 512, HD), BF16), vmem((1024, HD), BF16), vmem((32, HD), F32),
            vmem((4, 10, 16, HD), BF16), vmem((3, 10, 16, HD), BF16), vmem((1, HD), F32), vmem((3, 1, HD), F32),
            vmem((32, 16, HD), BF16), vmem((32, 1, HD), F32),
            vmem((10, 16, HD), BF16), vmem((7, 16, HD), BF16), vmem((256, HD), F32),
            vmem((8, 32, HD), BF16), vmem((15, 32, HD), BF16), vmem((1, HD), F32), vmem((15, 1, HD), F32),
            vmem((8, 16, HD), BF16), vmem((8, 16, HD), BF16), vmem((8, 16, HD), BF16),
            vmem((1, HD), F32), vmem((8, 1, HD), F32), vmem((64, HD), F32), vmem((64, HD), F32),
            vmem((32, 16, HD), BF16), vmem((8, 64, HD), BF16),
            pltpu.SemaphoreType.DMA((6,)), pltpu.SemaphoreType.DMA((14,)), pltpu.SemaphoreType.DMA((14,)),
            pltpu.SemaphoreType.REGULAR,
        ],
        compiler_params=pltpu.CompilerParams(
            collective_id=0, has_side_effects=True, vmem_limit_bytes=60 << 20
        ),
        name="attention_block",
    )(
        hidden_in, norm_gain, w_qkv.reshape(HD, 1280), qkv_bias, kv_pool.reshape(2, 512, HD),
        suffix_lengths, w_out,
    )


def solution(mesh):
    placed = (
        P(None, None, ("ctx", "grp")),
        P(("ctx", "grp")),
        P(("ctx", "grp"), "kvh", None),
        P("kvh", None),
        P("grp", None, "kvh", "ctx", None),
        P("ctx"),
        P("kvh", ("ctx", "grp")),
    )
    return jax.shard_map(
        local, mesh=mesh, in_specs=placed, out_specs=P(None, None, ("ctx", "grp")), check_vma=False
    )
```

```python
import functools
import math

import jax
import jax.numpy as jnp
from jax import lax
from jax.experimental import pallas as pl
from jax.experimental.pallas import tpu as pltpu
from jax.sharding import PartitionSpec as P

NORM_EPS = 1e-06
FLOOR_SCORE = -1e30
MESH = pl.DeviceIdType.MESH
NX, NY = 4, 8
HD = 128
F32, BF16 = jnp.float32, jnp.bfloat16


def zigzag(k, middle):
    return middle + (1 - 2 * lax.rem(k, 2)) * ((k + 1) // 2)


def wait_bytes(buffer, sem):
    pltpu.make_async_copy(buffer, buffer, sem).wait()


def total(parts):
    return functools.reduce(jnp.add, parts)


def kernel(
    h_any, gain_any, w_any, bias_any, kv_any, len_ref, wo_any, out_ref,
    h_v, gain_v, w_v, bias_v, kv_v, wo_v, head_bias, rows,
    part, part_in, sq, sq_in, direct_in, direct_sq_in,
    mid, mid_in, pairs, pairs_in, sq2, sq2_in,
    query, o_out, o_in, lse_out, lse_in, suf_out, suf_in, att, res,
    local_sem, send_sem, recv_sem, flag,
):
    ctx, kvh, grp = lax.axis_index("ctx"), lax.axis_index("kvh"), lax.axis_index("grp")
    x, y = ctx // NY, lax.rem(ctx, NY)
    z, core = kvh // 2, lax.rem(kvh, 2)
    lead = kvh - core + 1
    factor = 1.0 / math.sqrt(HD)
    first, late = grp == 0, grp == 1
    helper, worker = core == 0, core == 1

    def send(src, dst, phase, target):
        pltpu.make_async_remote_copy(
            src_ref=src, dst_ref=dst, send_sem=send_sem.at[phase], recv_sem=recv_sem.at[phase],
            device_id=target, device_id_type=MESH,
        ).start()

    loads = [
        pltpu.make_async_copy(src, dst, local_sem.at[i])
        for i, (src, dst) in enumerate(
            ((h_any, h_v), (gain_any, gain_v), (w_any, w_v), (bias_any, bias_v), (kv_any, kv_v.at[1, 3]), (wo_any, wo_v.at[1]))
        )
    ]
    for load in loads[:4]:
        load.start()

    def x_peer(i):
        return lax.rem(x + zigzag(i, 2), NX) * NY + y

    def y_peer(i):
        return lax.rem(y + zigzag(i, 4), NY)

    def column(to_y):
        return x * NY + to_y

    def plane_peer(i):
        return lax.rem(x + zigzag(lax.rem(i, 4), 2), NX), lax.rem(y + zigzag(i // 4, 4), NY)

    def z_peer(i):
        return lax.rem(z + 1 + i, 4) * 2

    barrier = pltpu.get_barrier_semaphore()

    def tell(sem, device):
        pl.semaphore_signal(sem, inc=1, device_id=device, device_id_type=MESH)

    hello, plane, go, ready, last = (flag.at[i] for i in range(5))

    @pl.when(worker)
    def _():
        @pl.loop(0, 3)
        def _(i):
            tell(barrier, {"ctx": x_peer(i)})

        @pl.loop(0, 4)
        def _(i):
            tell(barrier, {"ctx": x_peer(i), "kvh": lead - 1})

    @pl.when(worker & first)
    def _():
        @pl.loop(0, 7)
        def _(i):
            tell(barrier, {"ctx": column(y_peer(i))})

        @pl.loop(0, 3)
        def _(i):
            tell(barrier, {"kvh": z_peer(i) + 1})

    @pl.when(worker)
    def _():
        loads[4].start()
        loads[5].start()

    @pl.when(worker & first)
    def _():
        pl.semaphore_wait(barrier, 13)

        @pl.loop(0, 7)
        def _(i):
            tell(plane, {"ctx": column(y_peer(i))})

        pl.semaphore_wait(plane, 7)
        tell(barrier, {"grp": 1})
        tell(barrier, {"grp": 1, "kvh": lead - 1})

    @pl.when(helper & first)
    def _():
        pl.semaphore_wait(barrier, 4)

    loads[0].wait()
    loads[1].wait()
    h = h_v[...].astype(F32)
    h = jnp.concatenate([h[t, 8 * b : 8 * b + 8] for b in range(NX) for t in range(2)], axis=0)
    gain = gain_v[...].astype(F32).reshape(1, HD)
    scaled = (h * gain).astype(BF16)
    squares = jnp.sum(h * h, axis=1, keepdims=True)
    lane = lax.broadcasted_iota(jnp.int32, (64, HD), 1)
    row = lax.broadcasted_iota(jnp.int32, (64, HD), 0)
    sq[...] = jnp.sum(jnp.where(lane == row, squares, 0.0), axis=0, keepdims=True)
    loads[2].wait()
    for c in range(5):
        prod = jnp.dot(scaled, w_v[:, 256 * c : 256 * c + 256], preferred_element_type=F32).astype(BF16)
        for half in range(2):
            part[:, 2 * c + half] = prod[:, HD * half : HD * half + HD].reshape(NX, 16, HD)

    @pl.when(worker & late)
    def _():
        pl.semaphore_wait(barrier, 4)

        @pl.loop(0, 8)
        def _(i):
            tell(hello, {"ctx": column(y_peer(i)), "grp": 0})

    @pl.when(helper & late)
    def _():
        pl.semaphore_wait(barrier, 5)
        tell(hello, {"kvh": lead, "grp": 0})

    @pl.loop(0, 3)
    def _(i):
        to = x_peer(i)
        send(part.at[to // NY], part_in.at[core, i], 0, {"ctx": to, "kvh": lead})

    @pl.when(helper)
    def _():
        send(part.at[x], part_in.at[core, 3], 1, {"kvh": lead})

    @pl.when(worker)
    def _():
        @pl.loop(0, 3)
        def _(i):
            send(sq, sq_in.at[i], 8, {"ctx": x_peer(i)})

    @pl.when(late)
    def _():
        @pl.loop(0, 32)
        def _(i):
            to_x, to_y = plane_peer(i)
            send(part.at[to_x, to_y], direct_in.at[core, ctx], 6, {"ctx": to_x * NY + to_y, "kvh": lead, "grp": 0})

    @pl.when(late & worker)
    def _():
        @pl.loop(0, 32)
        def _(i):
            to_x, to_y = plane_peer(i)
            send(sq, direct_sq_in.at[ctx], 7, {"ctx": to_x * NY + to_y, "grp": 0})

    loads[3].wait()
    for j in range(8):
        head_bias[1, j : j + 1] = bias_v[:, HD * j : HD * j + HD].astype(F32)
    head_bias[1, 8:16] = head_bias[1, 0:8]
    head_bias[1, 16:24] = jnp.broadcast_to(bias_v[:, 8 * HD : 9 * HD].astype(F32), (8, HD))
    head_bias[1, 24:32] = jnp.broadcast_to(bias_v[:, 9 * HD :].astype(F32), (8, HD))

    @pl.when(helper)
    def _():
        own = {"kvh": lead}
        send(head_bias.at[1], head_bias.at[0], 2, own)

        @pl.when(late)
        def _():
            send(kv_any, kv_v.at[0, 3], 3, own)

    @pl.when(first)
    def _():
        @pl.loop(0, 3)
        def _(i):
            send(kv_any, kv_v.at[core, i], 4, {"ctx": x_peer(i), "kvh": lead})

    @pl.when(helper)
    def _():
        own = {"kvh": lead}

        @pl.when(first)
        def _():
            send(kv_any, kv_v.at[0, 3], 3, own)

        send(wo_any, wo_v.at[0], 5, own)

    @pl.when(worker)
    def _():
        rows[...] = jnp.zeros_like(rows)
        wait_bytes(sq_in, recv_sem.at[8])
        sq2[...] = total([sq_in[i] for i in range(3)]) + sq[...]
        wait_bytes(part_in.at[0, 3], recv_sem.at[1])
        wait_bytes(part_in.at[:, pl.ds(0, 3)], recv_sem.at[0])
        lines = [
            total([part_in[0, i].astype(F32) for i in range(4)]),
            total([part_in[1, i].astype(F32) for i in range(3)]) + part[x].astype(F32),
        ]

        @pl.when(first)
        def _():
            for head, line in enumerate(lines):
                mid[:, head] = line[0:8].astype(BF16)

            @pl.loop(0, 7)
            def _(i):
                to_y = y_peer(i)
                send(mid.at[to_y], mid_in.at[i], 9, {"ctx": column(to_y)})
                send(sq2, sq2_in.at[i], 10, {"ctx": column(to_y)})

        for head, line in enumerate(lines):
            rows[head, 0:144] = line[0:9].reshape(144, HD)
            rows[head, 192:208] = line[9]
            for b in range(8):
                pieces = [rows[head, pl.ds(b + at, 8, stride=step)] for at, step in ((0, 16), (8, 16), (128, 8), (192, 8))]
                pairs[b, head] = jnp.concatenate(pieces, axis=0).astype(BF16)

        @pl.when(first)
        def _():
            pl.semaphore_wait(hello, 9)
            tell(go, {"grp": 1})

            @pl.loop(0, 8)
            def _(i):
                to_y = y_peer(i)
                to = {"ctx": column(to_y), "grp": 1}
                send(pairs.at[to_y], pairs_in.at[7 + i], 11, to)
                send(sq2, sq2_in.at[7 + i], 10, to)

            @pl.loop(0, 3)
            def _(i):
                tell(ready, {"kvh": z_peer(i) + 1})

            lane = lax.broadcasted_iota(jnp.int32, (16, HD), 1)
            row = lax.broadcasted_iota(jnp.int32, (16, HD), 0)
            wait_bytes(sq2_in.at[pl.ds(0, 7)], recv_sem.at[10])
            wait_bytes(mid_in, recv_sem.at[9])
            wait_bytes(head_bias.at[0], recv_sem.at[2])
            squares = total([sq2_in[i] for i in range(7)]) + sq2[...]
            sums = [total([mid_in[i, head].astype(F32) for i in range(7)]) + mid[y, head].astype(F32) for head in range(2)]
            pl.semaphore_wait(ready, 3)
            tell(last, {"grp": 1})
            wait_bytes(direct_sq_in, recv_sem.at[7])
            squares = total([direct_sq_in[i] for i in range(32)]) + squares
            squares = jnp.sum(jnp.where(lane == row + 16 * x, squares, 0.0), axis=1, keepdims=True)
            inverse = lax.rsqrt(squares / 8192.0 + NORM_EPS)
            wait_bytes(direct_in, recv_sem.at[6])
            for head in range(2):
                summed = total([direct_in[head, i].astype(F32) for i in range(32)]) + sums[head]
                query[y, head] = (summed * inverse + head_bias[head, pl.ds(y, 1)]).astype(BF16)

            @pl.loop(0, 7)
            def _(i):
                send(query.at[y], query.at[y], 12, {"ctx": column(y_peer(i))})

        @pl.when(late)
        def _():
            pl.semaphore_wait(go, 1)

            @pl.loop(0, 7)
            def _(i):
                to_y = y_peer(i)
                send(pairs.at[to_y], pairs_in.at[i], 11, {"ctx": column(to_y)})
                send(sq2, sq2_in.at[i], 10, {"ctx": column(to_y)})

        loads[4].wait()

        def scores_of(q, keys):
            return lax.dot_general(q, keys, (((1,), (1,)), ((), ())), preferred_element_type=F32) * factor

        @pl.when(first)
        def _():
            lane = lax.broadcasted_iota(jnp.int32, (HD, HD), 1)
            row = lax.broadcasted_iota(jnp.int32, (HD, HD), 0)
            wait_bytes(kv_v.at[:, pl.ds(0, 3)], recv_sem.at[4])
            wait_bytes(kv_v.at[0, 3], recv_sem.at[3])
            wait_bytes(query.at[pl.ds(0, 7)], recv_sem.at[12])
            for head in range(2):
                q = query[:, head].reshape(HD, HD)
                scores = [scores_of(q, kv_v[head, i, 0]) for i in range(NX)]
                best = functools.reduce(jnp.maximum, [jnp.max(s, axis=1, keepdims=True) for s in scores])
                weights = [jnp.exp(s - best).astype(BF16) for s in scores]
                weight_sum = total([jnp.sum(w.astype(F32), axis=1, keepdims=True) for w in weights])
                out = total([jnp.dot(w, kv_v[head, i, 1], preferred_element_type=F32) for i, w in enumerate(weights)])
                o_out[:, head] = (out / weight_sum).astype(BF16).reshape(8, 16, HD)
                lse = best + jnp.log(weight_sum)
                lse_out[head] = jnp.sum(jnp.where(lane == row, lse, 0.0), axis=0, keepdims=True)

            @pl.loop(0, 15)
            def _(i):
                to_y, to_grp = y_peer(i // 2), 1 - lax.rem(i, 2)
                to = {"ctx": column(to_y), "grp": to_grp}
                send(o_out.at[to_y], o_in.at[y], 13, to)
                send(lse_out, lse_in.at[y], 14, to)

            o_in[y] = o_out[y]
            lse_in[y] = lse_out[...]

        @pl.when(late)
        def _():
            lane = lax.broadcasted_iota(jnp.int32, (32, HD), 1)
            row = lax.broadcasted_iota(jnp.int32, (32, HD), 0)
            step = jnp.where(row < 16, row // 8, lax.rem(row, 2))
            wait_bytes(head_bias.at[0], recv_sem.at[2])
            wait_bytes(kv_v.at[0, 3], recv_sem.at[3])
            wait_bytes(sq2_in, recv_sem.at[10])
            squares = total([sq2_in[i] for i in range(15)]) + sq2[...]
            squares = jnp.sum(jnp.where(lane == 16 * x + 8 * step + y, squares, 0.0), axis=1, keepdims=True)
            inverse = lax.rsqrt(squares / 8192.0 + NORM_EPS)
            wait_bytes(pairs_in, recv_sem.at[11])
            for head in range(2):
                summed = total([pairs_in[i, head].astype(F32) for i in range(15)]) + pairs[y, head].astype(F32)
                summed = (summed * inverse + head_bias[head]).astype(BF16)
                q = summed[0:16]
                fresh = summed[16:32]
                cached = scores_of(q, kv_v[head, 3, 0])
                slot = lax.broadcasted_iota(jnp.int32, cached.shape, 1)
                cached = jnp.where(slot < len_ref[0], cached, FLOOR_SCORE)
                new = scores_of(q, fresh)
                key_step = lax.broadcasted_iota(jnp.int32, new.shape, 1)
                q_step = lax.broadcasted_iota(jnp.int32, new.shape, 0) // 8
                new = jnp.where(key_step <= q_step, new, FLOOR_SCORE)
                best = jnp.maximum(jnp.max(cached, axis=1, keepdims=True), jnp.max(new, axis=1, keepdims=True))
                cached = jnp.exp(cached - best).astype(BF16)
                new = jnp.exp(new - best).astype(BF16)
                weight_sum = jnp.sum(cached.astype(F32), axis=1, keepdims=True) + jnp.sum(
                    new.astype(F32), axis=1, keepdims=True
                )
                out = jnp.dot(cached, kv_v[head, 3, 1], preferred_element_type=F32)
                values = jnp.concatenate([summed[24:32].astype(F32), jnp.zeros((8, HD), F32)], axis=0).astype(BF16)
                out = out + jnp.dot(new, values, preferred_element_type=F32)
                out = out / weight_sum
                lse = jnp.broadcast_to(best + jnp.log(weight_sum), (16, HD))
                for t in range(2):
                    suf_out[pl.ds(4 * head + t, 8, stride=8)] = out[8 * t : 8 * t + 8]
                    suf_out[pl.ds(4 * head + 2 + t, 8, stride=8)] = lse[8 * t : 8 * t + 8]

            mine = pl.ds(pl.multiple_of(8 * y, 8), 8)

            @pl.loop(0, 15)
            def _(i):
                to_y, to_grp = y_peer(i // 2), lax.rem(i, 2)
                to = {"ctx": column(to_y), "grp": to_grp}
                send(suf_out.at[pl.ds(pl.multiple_of(8 * to_y, 8), 8)], suf_in.at[mine], 15, to)

            suf_in[mine] = suf_out[mine]

        @pl.when(first)
        def _():
            wait_bytes(lse_in.at[pl.ds(0, 7)], recv_sem.at[14])
            wait_bytes(suf_in, recv_sem.at[15])
            wait_bytes(o_in.at[pl.ds(0, 7)], recv_sem.at[13])

        @pl.when(late)
        def _():
            wait_bytes(lse_in, recv_sem.at[14])
            wait_bytes(suf_in.at[pl.ds(0, 56)], recv_sem.at[15])
            wait_bytes(o_in, recv_sem.at[13])

        lane = lax.broadcasted_iota(jnp.int32, (16, HD), 1)
        row = lax.broadcasted_iota(jnp.int32, (16, HD), 0)
        mine = lane == row + 16 * y
        own = y * NX + x
        for head in range(2):
            lses = [jnp.sum(jnp.where(mine, lse_in[i, head], 0.0), axis=1, keepdims=True) for i in range(8)]
            lses.append(jnp.concatenate([suf_in[pl.ds(4 * head + 2 + t, 8, stride=8)] for t in range(2)], axis=0)[:, 0:1])
            best = functools.reduce(jnp.maximum, lses)
            shares = [jnp.exp(v - best) for v in lses]
            outs = [o_in[i, head].astype(F32) for i in range(8)]
            outs.append(jnp.concatenate([suf_in[pl.ds(4 * head + t, 8, stride=8)] for t in range(2)], axis=0))
            att[own, head] = (total([o * s for o, s in zip(outs, shares)]) / total(shares)).astype(BF16)

        @pl.loop(0, 31)
        def _(i):
            to_x, to_y = plane_peer(i)
            send(att.at[own], att.at[own], 16, {"ctx": to_x * NY + to_y})

        loads[5].wait()
        wait_bytes(wo_v.at[0], recv_sem.at[5])

        @pl.when(late)
        def _():
            pl.semaphore_wait(last, 1)

        wait_bytes(att.at[pl.ds(0, 31)], recv_sem.at[16])
        projected = total(
            [
                jnp.dot(
                    jnp.concatenate([att[4 * j : 4 * j + 4, head].reshape(64, HD) for head in range(2)], axis=1),
                    jnp.concatenate([wo_v[head, HD * j : HD * j + HD] for head in range(2)], axis=0),
                    preferred_element_type=F32,
                )
                for j in range(8)
            ]
        )
        ordered = [projected[16 * b + 8 * t : 16 * b + 8 * t + 8] for t in range(2) for b in range(NX)]
        res[z] = jnp.concatenate(ordered, axis=0).astype(BF16)

        @pl.loop(0, 3)
        def _(i):
            send(res.at[z], res.at[z], 17, {"kvh": z_peer(i)})
            send(res.at[z], res.at[z], 17, {"kvh": z_peer(i) + 1})

        send(res.at[z], res.at[z], 17, {"kvh": lead - 1})

    wait_bytes(part_in.at[0, pl.ds(0, 3)], send_sem.at[0])

    @pl.when(first)
    def _():
        wait_bytes(kv_v.at[0, pl.ds(0, 3)], send_sem.at[4])

    @pl.when(late)
    def _():
        wait_bytes(direct_in.at[0], send_sem.at[6])

    @pl.when(helper)
    def _():
        wait_bytes(part_in.at[0, 3], send_sem.at[1])
        wait_bytes(head_bias.at[0], send_sem.at[2])
        wait_bytes(kv_v.at[0, 3], send_sem.at[3])
        wait_bytes(wo_v.at[0], send_sem.at[5])

    @pl.when(worker)
    def _():
        wait_bytes(sq_in, send_sem.at[8])

        @pl.when(first)
        def _():
            wait_bytes(mid_in, send_sem.at[9])
            wait_bytes(sq2_in, send_sem.at[10])
            wait_bytes(pairs_in.at[pl.ds(0, 8)], send_sem.at[11])
            wait_bytes(query.at[pl.ds(0, 7)], send_sem.at[12])
            wait_bytes(o_in, send_sem.at[13])
            wait_bytes(o_in.at[pl.ds(0, 7)], send_sem.at[13])
            wait_bytes(lse_in, send_sem.at[14])
            wait_bytes(lse_in.at[pl.ds(0, 7)], send_sem.at[14])

        @pl.when(late)
        def _():
            wait_bytes(direct_sq_in, send_sem.at[7])
            wait_bytes(sq2_in.at[pl.ds(0, 7)], send_sem.at[10])
            wait_bytes(pairs_in.at[pl.ds(0, 7)], send_sem.at[11])
            wait_bytes(suf_in, send_sem.at[15])
            wait_bytes(suf_in.at[pl.ds(0, 56)], send_sem.at[15])

        wait_bytes(att.at[pl.ds(0, 31)], send_sem.at[16])
        wait_bytes(res, send_sem.at[17])
        wait_bytes(res.at[pl.ds(0, 3)], send_sem.at[17])
        wait_bytes(res.at[pl.ds(0, 3)], recv_sem.at[17])

    @pl.when(helper)
    def _():
        wait_bytes(res, recv_sem.at[17])

    out_ref[...] = total([res[k].astype(F32) for k in range(4)]).astype(BF16).reshape(2, 32, HD)


def local(hidden_in, norm_gain, w_qkv, qkv_bias, kv_pool, suffix_lengths, w_out):
    anywhere = pl.BlockSpec(memory_space=pl.ANY)
    vmem = pltpu.VMEM
    return pl.pallas_call(
        kernel,
        out_shape=jax.ShapeDtypeStruct((2, 32, HD), BF16),
        in_specs=[anywhere] * 5 + [pl.BlockSpec(memory_space=pltpu.SMEM), anywhere],
        out_specs=pl.BlockSpec(memory_space=vmem),
        scratch_shapes=[
            vmem((2, 32, HD), BF16), vmem((HD,), BF16), vmem((HD, 1280), BF16), vmem((1, 1280), BF16),
            vmem((2, 4, 2, 512, HD), BF16), vmem((2, 1024, HD), BF16), vmem((2, 32, HD), F32), vmem((2, 256, HD), F32),
            vmem((4, 10, 16, HD), BF16), vmem((2, 4, 10, 16, HD), BF16), vmem((1, HD), F32), vmem((3, 1, HD), F32),
            vmem((2, 32, 16, HD), BF16), vmem((32, 1, HD), F32),
            vmem((8, 2, 16, HD), BF16), vmem((7, 2, 16, HD), BF16),
            vmem((8, 2, 32, HD), BF16), vmem((15, 2, 32, HD), BF16), vmem((1, HD), F32), vmem((15, 1, HD), F32),
            vmem((8, 2, 16, HD), BF16), vmem((8, 2, 16, HD), BF16), vmem((8, 2, 16, HD), BF16),
            vmem((2, 1, HD), F32), vmem((8, 2, 1, HD), F32), vmem((64, HD), F32), vmem((64, HD), F32),
            vmem((32, 2, 16, HD), BF16), vmem((4, 64, HD), BF16),
            pltpu.SemaphoreType.DMA((6,)), pltpu.SemaphoreType.DMA((18,)), pltpu.SemaphoreType.DMA((18,)),
            pltpu.SemaphoreType.REGULAR((5,)),
        ],
        compiler_params=pltpu.CompilerParams(
            collective_id=0, has_side_effects=True, vmem_limit_bytes=60 << 20
        ),
        name="attention_block",
    )(
        hidden_in, norm_gain, w_qkv.reshape(HD, 1280), qkv_bias, kv_pool.reshape(2, 512, HD),
        suffix_lengths, w_out,
    )


def solution(mesh):
    placed = (
        P(None, None, ("ctx", "grp")),
        P(("ctx", "grp")),
        P(("ctx", "grp"), "kvh", None),
        P("kvh", None),
        P("grp", None, "kvh", "ctx", None),
        P("ctx"),
        P("kvh", ("ctx", "grp")),
    )
    return jax.shard_map(
        local, mesh=mesh, in_specs=placed, out_specs=P(None, None, ("ctx", "grp")), check_vma=False
    )
```

```python
import functools
import math

import jax
import jax.numpy as jnp
from jax import lax
from jax.experimental import pallas as pl
from jax.experimental.pallas import tpu as pltpu
from jax.sharding import PartitionSpec as P

NORM_EPS = 1e-06
FLOOR_SCORE = -1e30
MESH = pl.DeviceIdType.MESH
NX, NY = 4, 8
HD = 128
F32, BF16 = jnp.float32, jnp.bfloat16


def zigzag(k, middle):
    if isinstance(k, int):
        return middle + (1 - 2 * (k % 2)) * ((k + 1) // 2)
    return middle + (1 - 2 * lax.rem(k, 2)) * ((k + 1) // 2)


def wait_bytes(buffer, sem):
    pltpu.make_async_copy(buffer, buffer, sem).wait()


def total(parts):
    return functools.reduce(jnp.add, parts)


def kernel(
    h_any, gain_any, w_any, bias_any, kv_any, len_any, wo_any, out_ref,
    h_v, gain_v, w_v, bias_v, kv_v, wo_v, len_ref, head_bias, rows,
    part, part_in, sq, sq_in, direct_in, direct_sq_in,
    mid, mid_in, pairs, pairs_in, sq2, sq2_in,
    query, o_out, o_in, lse_out, lse_in, suf_out, suf_in, att, res,
    local_sem, send_sem, recv_sem, flag,
):
    ctx, kvh, grp = lax.axis_index("ctx"), lax.axis_index("kvh"), lax.axis_index("grp")
    x, y = ctx // NY, lax.rem(ctx, NY)
    z, core = kvh // 2, lax.rem(kvh, 2)
    lead = kvh - core + 1
    factor = 1.0 / math.sqrt(HD)
    first, late = grp == 0, grp == 1
    helper, worker = core == 0, core == 1

    def send(src, dst, phase, target):
        pltpu.make_async_remote_copy(
            src_ref=src, dst_ref=dst, send_sem=send_sem.at[phase], recv_sem=recv_sem.at[phase],
            device_id=target, device_id_type=MESH,
        ).start()

    loads = [
        pltpu.make_async_copy(src, dst, local_sem.at[i])
        for i, (src, dst) in enumerate(
            ((h_any, h_v), (gain_any, gain_v), (w_any, w_v), (bias_any, bias_v), (kv_any, kv_v.at[1, 3]), (wo_any, wo_v.at[1]), (len_any, len_ref))
        )
    ]
    for load in loads[:4]:
        load.start()

    def x_peer(i):
        return lax.rem(x + zigzag(i, 2), NX) * NY + y

    def y_peer(i):
        return lax.rem(y + zigzag(i, 4), NY)

    def column(to_y):
        return x * NY + to_y

    def plane_peer(i):
        return lax.rem(x + zigzag(lax.rem(i, 4), 2), NX), lax.rem(y + zigzag(i // 4, 4), NY)

    def z_peer(i):
        return lax.rem(z + 1 + i, 4) * 2

    barrier = pltpu.get_barrier_semaphore()

    def tell(sem, device):
        pl.semaphore_signal(sem, inc=1, device_id=device, device_id_type=MESH)

    hello, plane, go, ready, last = (flag.at[i] for i in range(5))

    @pl.when(worker)
    def _():
        @pl.loop(0, 3, unroll=True)
        def _(i):
            tell(barrier, {"ctx": x_peer(i)})

        @pl.loop(0, 4, unroll=True)
        def _(i):
            tell(barrier, {"ctx": x_peer(i), "kvh": lead - 1})

    @pl.when(worker & first)
    def _():
        @pl.loop(0, 7, unroll=True)
        def _(i):
            tell(barrier, {"ctx": column(y_peer(i))})

        @pl.loop(0, 3, unroll=True)
        def _(i):
            tell(barrier, {"kvh": z_peer(i) + 1})

    @pl.when(worker)
    def _():
        loads[4].start()
        loads[5].start()
        loads[6].start()

    @pl.when(worker & first)
    def _():
        pl.semaphore_wait(barrier, 13)

        @pl.loop(0, 7, unroll=True)
        def _(i):
            tell(plane, {"ctx": column(y_peer(i))})

        pl.semaphore_wait(plane, 7)
        tell(barrier, {"grp": 1})
        tell(barrier, {"grp": 1, "kvh": lead - 1})

    @pl.when(helper & first)
    def _():
        pl.semaphore_wait(barrier, 4)

    loads[0].wait()
    loads[1].wait()
    h = h_v[...].astype(F32)
    h = jnp.concatenate([h[t, 8 * b : 8 * b + 8] for b in range(NX) for t in range(2)], axis=0)
    gain = gain_v[...].astype(F32).reshape(1, HD)
    scaled = (h * gain).astype(BF16)
    squares = jnp.sum(h * h, axis=1, keepdims=True)
    lane = lax.broadcasted_iota(jnp.int32, (64, HD), 1)
    row = lax.broadcasted_iota(jnp.int32, (64, HD), 0)
    sq[...] = jnp.sum(jnp.where(lane == row, squares, 0.0), axis=0, keepdims=True)
    loads[2].wait()
    for c in range(5):
        prod = jnp.dot(scaled, w_v[:, 256 * c : 256 * c + 256], preferred_element_type=F32).astype(BF16)
        for half in range(2):
            part[:, 2 * c + half] = prod[:, HD * half : HD * half + HD].reshape(NX, 16, HD)

    @pl.when(worker & late)
    def _():
        pl.semaphore_wait(barrier, 4)

        @pl.loop(0, 8, unroll=True)
        def _(i):
            tell(hello, {"ctx": column(y_peer(i)), "grp": 0})

    @pl.when(helper & late)
    def _():
        pl.semaphore_wait(barrier, 5)
        tell(hello, {"kvh": lead, "grp": 0})

    @pl.loop(0, 3, unroll=True)
    def _(i):
        to = x_peer(i)
        send(part.at[to // NY], part_in.at[core, i], 0, {"ctx": to, "kvh": lead})

    @pl.when(helper)
    def _():
        send(part.at[x], part_in.at[core, 3], 1, {"kvh": lead})

    @pl.when(worker)
    def _():
        @pl.loop(0, 3, unroll=True)
        def _(i):
            send(sq, sq_in.at[i], 8, {"ctx": x_peer(i)})

    @pl.when(late)
    def _():
        @pl.loop(0, 32, unroll=True)
        def _(i):
            to_x, to_y = plane_peer(i)
            send(part.at[to_x, to_y], direct_in.at[core, ctx], 6, {"ctx": to_x * NY + to_y, "kvh": lead, "grp": 0})

    @pl.when(late & worker)
    def _():
        @pl.loop(0, 32, unroll=True)
        def _(i):
            to_x, to_y = plane_peer(i)
            send(sq, direct_sq_in.at[ctx], 7, {"ctx": to_x * NY + to_y, "grp": 0})

    loads[3].wait()
    for j in range(8):
        head_bias[1, j : j + 1] = bias_v[:, HD * j : HD * j + HD].astype(F32)
    head_bias[1, 8:16] = head_bias[1, 0:8]
    head_bias[1, 16:24] = jnp.broadcast_to(bias_v[:, 8 * HD : 9 * HD].astype(F32), (8, HD))
    head_bias[1, 24:32] = jnp.broadcast_to(bias_v[:, 9 * HD :].astype(F32), (8, HD))

    @pl.when(helper)
    def _():
        own = {"kvh": lead}
        send(head_bias.at[1], head_bias.at[0], 2, own)

        @pl.when(late)
        def _():
            send(kv_any, kv_v.at[0, 3], 3, own)

    @pl.when(first)
    def _():
        @pl.loop(0, 3, unroll=True)
        def _(i):
            send(kv_any, kv_v.at[core, i], 4, {"ctx": x_peer(i), "kvh": lead})

    @pl.when(helper)
    def _():
        own = {"kvh": lead}

        @pl.when(first)
        def _():
            send(kv_any, kv_v.at[0, 3], 3, own)

        send(wo_any, wo_v.at[0], 5, own)

    @pl.when(worker)
    def _():
        rows[...] = jnp.zeros_like(rows)
        wait_bytes(sq_in, recv_sem.at[8])
        sq2[...] = total([sq_in[i] for i in range(3)]) + sq[...]
        wait_bytes(part_in.at[0, 3], recv_sem.at[1])
        wait_bytes(part_in.at[:, pl.ds(0, 3)], recv_sem.at[0])
        lines = [
            total([part_in[0, i].astype(F32) for i in range(4)]),
            total([part_in[1, i].astype(F32) for i in range(3)]) + part[x].astype(F32),
        ]

        @pl.when(first)
        def _():
            for head, line in enumerate(lines):
                mid[:, head] = line[0:8].astype(BF16)

            @pl.loop(0, 7, unroll=True)
            def _(i):
                to_y = y_peer(i)
                send(mid.at[to_y], mid_in.at[i], 9, {"ctx": column(to_y)})
                send(sq2, sq2_in.at[i], 10, {"ctx": column(to_y)})

        for head, line in enumerate(lines):
            rows[head, 0:144] = line[0:9].reshape(144, HD)
            rows[head, 192:208] = line[9]
            for b in range(8):
                pieces = [rows[head, pl.ds(b + at, 8, stride=step)] for at, step in ((0, 16), (8, 16), (128, 8), (192, 8))]
                pairs[b, head] = jnp.concatenate(pieces, axis=0).astype(BF16)

        @pl.when(first)
        def _():
            pl.semaphore_wait(hello, 9)
            tell(go, {"grp": 1})

            @pl.loop(0, 8, unroll=True)
            def _(i):
                to_y = y_peer(i)
                to = {"ctx": column(to_y), "grp": 1}
                send(pairs.at[to_y], pairs_in.at[7 + i], 11, to)
                send(sq2, sq2_in.at[7 + i], 10, to)

            @pl.loop(0, 3, unroll=True)
            def _(i):
                tell(ready, {"kvh": z_peer(i) + 1})

            lane = lax.broadcasted_iota(jnp.int32, (16, HD), 1)
            row = lax.broadcasted_iota(jnp.int32, (16, HD), 0)
            wait_bytes(sq2_in.at[pl.ds(0, 7)], recv_sem.at[10])
            wait_bytes(mid_in, recv_sem.at[9])
            wait_bytes(head_bias.at[0], recv_sem.at[2])
            squares = total([sq2_in[i] for i in range(7)]) + sq2[...]
            sums = [total([mid_in[i, head].astype(F32) for i in range(7)]) + mid[y, head].astype(F32) for head in range(2)]
            pl.semaphore_wait(ready, 3)
            tell(last, {"grp": 1})
            wait_bytes(direct_sq_in, recv_sem.at[7])
            squares = total([direct_sq_in[i] for i in range(32)]) + squares
            squares = jnp.sum(jnp.where(lane == row + 16 * x, squares, 0.0), axis=1, keepdims=True)
            inverse = lax.rsqrt(squares / 8192.0 + NORM_EPS)
            wait_bytes(direct_in, recv_sem.at[6])
            for head in range(2):
                summed = total([direct_in[head, i].astype(F32) for i in range(32)]) + sums[head]
                query[y, head] = (summed * inverse + head_bias[head, pl.ds(y, 1)]).astype(BF16)

            @pl.loop(0, 7, unroll=True)
            def _(i):
                send(query.at[y], query.at[y], 12, {"ctx": column(y_peer(i))})

        @pl.when(late)
        def _():
            pl.semaphore_wait(go, 1)

            @pl.loop(0, 7, unroll=True)
            def _(i):
                to_y = y_peer(i)
                send(pairs.at[to_y], pairs_in.at[i], 11, {"ctx": column(to_y)})
                send(sq2, sq2_in.at[i], 10, {"ctx": column(to_y)})

        loads[4].wait()
        loads[6].wait()

        def scores_of(q, keys):
            return lax.dot_general(q, keys, (((1,), (1,)), ((), ())), preferred_element_type=F32) * factor

        @pl.when(first)
        def _():
            lane = lax.broadcasted_iota(jnp.int32, (HD, HD), 1)
            row = lax.broadcasted_iota(jnp.int32, (HD, HD), 0)
            wait_bytes(kv_v.at[:, pl.ds(0, 3)], recv_sem.at[4])
            wait_bytes(kv_v.at[0, 3], recv_sem.at[3])
            wait_bytes(query.at[pl.ds(0, 7)], recv_sem.at[12])
            for head in range(2):
                q = query[:, head].reshape(HD, HD)
                scores = [scores_of(q, kv_v[head, i, 0]) for i in range(NX)]
                best = functools.reduce(jnp.maximum, [jnp.max(s, axis=1, keepdims=True) for s in scores])
                weights = [jnp.exp(s - best).astype(BF16) for s in scores]
                weight_sum = total([jnp.sum(w.astype(F32), axis=1, keepdims=True) for w in weights])
                out = total([jnp.dot(w, kv_v[head, i, 1], preferred_element_type=F32) for i, w in enumerate(weights)])
                o_out[:, head] = (out / weight_sum).astype(BF16).reshape(8, 16, HD)
                lse = best + jnp.log(weight_sum)
                lse_out[head] = jnp.sum(jnp.where(lane == row, lse, 0.0), axis=0, keepdims=True)

            @pl.loop(0, 15, unroll=True)
            def _(i):
                to_y, to_grp = y_peer(i // 2), 1 - lax.rem(i, 2)
                to = {"ctx": column(to_y), "grp": to_grp}
                send(o_out.at[to_y], o_in.at[y], 13, to)
                send(lse_out, lse_in.at[y], 14, to)

            o_in[y] = o_out[y]
            lse_in[y] = lse_out[...]

        @pl.when(late)
        def _():
            lane = lax.broadcasted_iota(jnp.int32, (32, HD), 1)
            row = lax.broadcasted_iota(jnp.int32, (32, HD), 0)
            step = jnp.where(row < 16, row // 8, lax.rem(row, 2))
            wait_bytes(head_bias.at[0], recv_sem.at[2])
            wait_bytes(kv_v.at[0, 3], recv_sem.at[3])
            wait_bytes(sq2_in, recv_sem.at[10])
            squares = total([sq2_in[i] for i in range(15)]) + sq2[...]
            squares = jnp.sum(jnp.where(lane == 16 * x + 8 * step + y, squares, 0.0), axis=1, keepdims=True)
            inverse = lax.rsqrt(squares / 8192.0 + NORM_EPS)
            wait_bytes(pairs_in, recv_sem.at[11])
            for head in range(2):
                summed = total([pairs_in[i, head].astype(F32) for i in range(15)]) + pairs[y, head].astype(F32)
                summed = (summed * inverse + head_bias[head]).astype(BF16)
                q = summed[0:16]
                fresh = summed[16:32]
                cached = scores_of(q, kv_v[head, 3, 0])
                slot = lax.broadcasted_iota(jnp.int32, cached.shape, 1)
                cached = jnp.where(slot < len_ref[0], cached, FLOOR_SCORE)
                new = scores_of(q, fresh)
                key_step = lax.broadcasted_iota(jnp.int32, new.shape, 1)
                q_step = lax.broadcasted_iota(jnp.int32, new.shape, 0) // 8
                new = jnp.where(key_step <= q_step, new, FLOOR_SCORE)
                best = jnp.maximum(jnp.max(cached, axis=1, keepdims=True), jnp.max(new, axis=1, keepdims=True))
                cached = jnp.exp(cached - best).astype(BF16)
                new = jnp.exp(new - best).astype(BF16)
                weight_sum = jnp.sum(cached.astype(F32), axis=1, keepdims=True) + jnp.sum(
                    new.astype(F32), axis=1, keepdims=True
                )
                out = jnp.dot(cached, kv_v[head, 3, 1], preferred_element_type=F32)
                values = jnp.concatenate([summed[24:32].astype(F32), jnp.zeros((8, HD), F32)], axis=0).astype(BF16)
                out = out + jnp.dot(new, values, preferred_element_type=F32)
                out = out / weight_sum
                lse = jnp.broadcast_to(best + jnp.log(weight_sum), (16, HD))
                for t in range(2):
                    suf_out[pl.ds(4 * head + t, 8, stride=8)] = out[8 * t : 8 * t + 8]
                    suf_out[pl.ds(4 * head + 2 + t, 8, stride=8)] = lse[8 * t : 8 * t + 8]

            mine = pl.ds(pl.multiple_of(8 * y, 8), 8)

            @pl.loop(0, 15, unroll=True)
            def _(i):
                to_y, to_grp = y_peer(i // 2), lax.rem(i, 2)
                to = {"ctx": column(to_y), "grp": to_grp}
                send(suf_out.at[pl.ds(pl.multiple_of(8 * to_y, 8), 8)], suf_in.at[mine], 15, to)

            suf_in[mine] = suf_out[mine]

        @pl.when(first)
        def _():
            wait_bytes(lse_in.at[pl.ds(0, 7)], recv_sem.at[14])
            wait_bytes(suf_in, recv_sem.at[15])
            wait_bytes(o_in.at[pl.ds(0, 7)], recv_sem.at[13])

        @pl.when(late)
        def _():
            wait_bytes(lse_in, recv_sem.at[14])
            wait_bytes(suf_in.at[pl.ds(0, 56)], recv_sem.at[15])
            wait_bytes(o_in, recv_sem.at[13])

        lane = lax.broadcasted_iota(jnp.int32, (16, HD), 1)
        row = lax.broadcasted_iota(jnp.int32, (16, HD), 0)
        mine = lane == row + 16 * y
        own = y * NX + x
        for head in range(2):
            lses = [jnp.sum(jnp.where(mine, lse_in[i, head], 0.0), axis=1, keepdims=True) for i in range(8)]
            lses.append(jnp.concatenate([suf_in[pl.ds(4 * head + 2 + t, 8, stride=8)] for t in range(2)], axis=0)[:, 0:1])
            best = functools.reduce(jnp.maximum, lses)
            shares = [jnp.exp(v - best) for v in lses]
            outs = [o_in[i, head].astype(F32) for i in range(8)]
            outs.append(jnp.concatenate([suf_in[pl.ds(4 * head + t, 8, stride=8)] for t in range(2)], axis=0))
            att[own, head] = (total([o * s for o, s in zip(outs, shares)]) / total(shares)).astype(BF16)

        @pl.loop(0, 31, unroll=True)
        def _(i):
            to_x, to_y = plane_peer(i)
            send(att.at[own], att.at[own], 16, {"ctx": to_x * NY + to_y})

        loads[5].wait()
        wait_bytes(wo_v.at[0], recv_sem.at[5])

        @pl.when(late)
        def _():
            pl.semaphore_wait(last, 1)

        wait_bytes(att.at[pl.ds(0, 31)], recv_sem.at[16])
        projected = total(
            [
                jnp.dot(
                    jnp.concatenate([att[4 * j : 4 * j + 4, head].reshape(64, HD) for head in range(2)], axis=1),
                    jnp.concatenate([wo_v[head, HD * j : HD * j + HD] for head in range(2)], axis=0),
                    preferred_element_type=F32,
                )
                for j in range(8)
            ]
        )
        ordered = [projected[16 * b + 8 * t : 16 * b + 8 * t + 8] for t in range(2) for b in range(NX)]
        res[z] = jnp.concatenate(ordered, axis=0).astype(BF16)

        @pl.loop(0, 3, unroll=True)
        def _(i):
            send(res.at[z], res.at[z], 17, {"kvh": z_peer(i)})
            send(res.at[z], res.at[z], 17, {"kvh": z_peer(i) + 1})

        send(res.at[z], res.at[z], 17, {"kvh": lead - 1})

    wait_bytes(part_in.at[0, pl.ds(0, 3)], send_sem.at[0])

    @pl.when(first)
    def _():
        wait_bytes(kv_v.at[0, pl.ds(0, 3)], send_sem.at[4])

    @pl.when(late)
    def _():
        wait_bytes(direct_in.at[0], send_sem.at[6])

    @pl.when(helper)
    def _():
        wait_bytes(part_in.at[0, 3], send_sem.at[1])
        wait_bytes(head_bias.at[0], send_sem.at[2])
        wait_bytes(kv_v.at[0, 3], send_sem.at[3])
        wait_bytes(wo_v.at[0], send_sem.at[5])

    @pl.when(worker)
    def _():
        wait_bytes(sq_in, send_sem.at[8])

        @pl.when(first)
        def _():
            wait_bytes(mid_in, send_sem.at[9])
            wait_bytes(sq2_in, send_sem.at[10])
            wait_bytes(pairs_in.at[pl.ds(0, 8)], send_sem.at[11])
            wait_bytes(query.at[pl.ds(0, 7)], send_sem.at[12])
            wait_bytes(o_in, send_sem.at[13])
            wait_bytes(o_in.at[pl.ds(0, 7)], send_sem.at[13])
            wait_bytes(lse_in, send_sem.at[14])
            wait_bytes(lse_in.at[pl.ds(0, 7)], send_sem.at[14])

        @pl.when(late)
        def _():
            wait_bytes(direct_sq_in, send_sem.at[7])
            wait_bytes(sq2_in.at[pl.ds(0, 7)], send_sem.at[10])
            wait_bytes(pairs_in.at[pl.ds(0, 7)], send_sem.at[11])
            wait_bytes(suf_in, send_sem.at[15])
            wait_bytes(suf_in.at[pl.ds(0, 56)], send_sem.at[15])

        wait_bytes(att.at[pl.ds(0, 31)], send_sem.at[16])
        wait_bytes(res, send_sem.at[17])
        wait_bytes(res.at[pl.ds(0, 3)], send_sem.at[17])
        wait_bytes(res.at[pl.ds(0, 3)], recv_sem.at[17])

    @pl.when(helper)
    def _():
        wait_bytes(res, recv_sem.at[17])

    out_ref[...] = total([res[k].astype(F32) for k in range(4)]).astype(BF16).reshape(2, 32, HD)


def local(hidden_in, norm_gain, w_qkv, qkv_bias, kv_pool, suffix_lengths, w_out):
    anywhere = pl.BlockSpec(memory_space=pl.ANY)
    vmem = pltpu.VMEM
    return pl.pallas_call(
        kernel,
        out_shape=jax.ShapeDtypeStruct((2, 32, HD), BF16),
        in_specs=[anywhere] * 7,
        out_specs=pl.BlockSpec(memory_space=vmem),
        scratch_shapes=[
            vmem((2, 32, HD), BF16), vmem((HD,), BF16), vmem((HD, 1280), BF16), vmem((1, 1280), BF16),
            vmem((2, 4, 2, 512, HD), BF16), vmem((2, 1024, HD), BF16), pltpu.SMEM((1,), jnp.int32), vmem((2, 32, HD), F32), vmem((2, 256, HD), F32),
            vmem((4, 10, 16, HD), BF16), vmem((2, 4, 10, 16, HD), BF16), vmem((1, HD), F32), vmem((3, 1, HD), F32),
            vmem((2, 32, 16, HD), BF16), vmem((32, 1, HD), F32),
            vmem((8, 2, 16, HD), BF16), vmem((7, 2, 16, HD), BF16),
            vmem((8, 2, 32, HD), BF16), vmem((15, 2, 32, HD), BF16), vmem((1, HD), F32), vmem((15, 1, HD), F32),
            vmem((8, 2, 16, HD), BF16), vmem((8, 2, 16, HD), BF16), vmem((8, 2, 16, HD), BF16),
            vmem((2, 1, HD), F32), vmem((8, 2, 1, HD), F32), vmem((64, HD), F32), vmem((64, HD), F32),
            vmem((32, 2, 16, HD), BF16), vmem((4, 64, HD), BF16),
            pltpu.SemaphoreType.DMA((7,)), pltpu.SemaphoreType.DMA((18,)), pltpu.SemaphoreType.DMA((18,)),
            pltpu.SemaphoreType.REGULAR((5,)),
        ],
        compiler_params=pltpu.CompilerParams(
            collective_id=0, has_side_effects=True, vmem_limit_bytes=60 << 20
        ),
        name="attention_block",
    )(
        hidden_in, norm_gain, w_qkv.reshape(HD, 1280), qkv_bias, kv_pool.reshape(2, 512, HD),
        suffix_lengths, w_out,
    )


def solution(mesh):
    placed = (
        P(None, None, ("ctx", "grp")),
        P(("ctx", "grp")),
        P(("ctx", "grp"), "kvh", None),
        P("kvh", None),
        P("grp", None, "kvh", "ctx", None),
        P("ctx"),
        P("kvh", ("ctx", "grp")),
    )
    return jax.shard_map(
        local, mesh=mesh, in_specs=placed, out_specs=P(None, None, ("ctx", "grp")), check_vma=False
    )
```

```python
import functools
import math

import jax
import jax.numpy as jnp
from jax import lax
from jax.experimental import pallas as pl
from jax.experimental.pallas import tpu as pltpu
from jax.sharding import PartitionSpec as P

NORM_EPS = 1e-06
FLOOR_SCORE = -1e30
MESH = pl.DeviceIdType.MESH
NX, NY = 4, 8
HD = 128
F32, BF16 = jnp.float32, jnp.bfloat16


def zigzag(k, middle):
    if isinstance(k, int):
        return middle + (1 - 2 * (k % 2)) * ((k + 1) // 2)
    return middle + (1 - 2 * lax.rem(k, 2)) * ((k + 1) // 2)


def wait_bytes(buffer, sem):
    pltpu.make_async_copy(buffer, buffer, sem).wait()


def total(parts):
    return functools.reduce(jnp.add, parts)


def kernel(
    h_any, gain_any, w_any, bias_any, kv_any, len_any, wo_any, out_ref,
    h_v, gain_v, w_v, bias_v, kv_v, wo_v, len_ref, head_bias, rows,
    part, part_in, sq, sq_in, direct_in, direct_sq_in,
    mid, mid_in, pairs, pairs_in, sq2, sq2_in,
    query, o_out, o_in, lse_out, lse_in, suf_out, suf_in, att, res,
    local_sem, send_sem, recv_sem, flag,
):
    ctx, kvh, grp = lax.axis_index("ctx"), lax.axis_index("kvh"), lax.axis_index("grp")
    x, y = ctx // NY, lax.rem(ctx, NY)
    z, core = kvh // 2, lax.rem(kvh, 2)
    lead = kvh - core + 1
    factor = 1.0 / math.sqrt(HD)
    first, late = grp == 0, grp == 1
    helper, worker = core == 0, core == 1

    def send(src, dst, phase, target):
        pltpu.make_async_remote_copy(
            src_ref=src, dst_ref=dst, send_sem=send_sem.at[phase], recv_sem=recv_sem.at[phase],
            device_id=target, device_id_type=MESH,
        ).start()

    loads = [
        pltpu.make_async_copy(src, dst, local_sem.at[i])
        for i, (src, dst) in enumerate(
            ((h_any, h_v), (gain_any, gain_v), (w_any, w_v), (bias_any, bias_v), (kv_any, kv_v.at[1, 3]), (wo_any, wo_v.at[1]), (len_any, len_ref))
        )
    ]
    for load in loads[:4]:
        load.start()

    def x_peer(i):
        return lax.rem(x + zigzag(i, 2), NX) * NY + y

    def y_peer(i):
        return lax.rem(y + zigzag(i, 4), NY)

    def column(to_y):
        return x * NY + to_y

    def plane_peer(i):
        return lax.rem(x + zigzag(lax.rem(i, 4), 2), NX), lax.rem(y + zigzag(i // 4, 4), NY)

    def z_peer(i):
        return lax.rem(z + 1 + i, 4) * 2

    barrier = pltpu.get_barrier_semaphore()

    def tell(sem, device):
        pl.semaphore_signal(sem, inc=1, device_id=device, device_id_type=MESH)

    hello, plane, go, ready, last = (flag.at[i] for i in range(5))

    @pl.when(worker)
    def _():
        @pl.loop(0, 3, unroll=True)
        def _(i):
            tell(barrier, {"ctx": x_peer(i)})

        @pl.loop(0, 4, unroll=True)
        def _(i):
            tell(barrier, {"ctx": x_peer(i), "kvh": lead - 1})

    @pl.when(worker & first)
    def _():
        @pl.loop(0, 7, unroll=True)
        def _(i):
            tell(barrier, {"ctx": column(y_peer(i))})

        @pl.loop(0, 3, unroll=True)
        def _(i):
            tell(barrier, {"kvh": z_peer(i) + 1})

    @pl.when(worker)
    def _():
        loads[4].start()
        loads[5].start()
        loads[6].start()

    @pl.when(worker & first)
    def _():
        pl.semaphore_wait(barrier, 13)

        @pl.loop(0, 7, unroll=True)
        def _(i):
            tell(plane, {"ctx": column(y_peer(i))})

        pl.semaphore_wait(plane, 7)
        tell(barrier, {"grp": 1})
        tell(barrier, {"grp": 1, "kvh": lead - 1})

    @pl.when(helper & first)
    def _():
        pl.semaphore_wait(barrier, 4)

    loads[0].wait()
    loads[1].wait()
    h = h_v[...].astype(F32)
    h = jnp.concatenate([h[t, 8 * b : 8 * b + 8] for b in range(NX) for t in range(2)], axis=0)
    gain = gain_v[...].astype(F32).reshape(1, HD)
    scaled = (h * gain).astype(BF16)
    squares = jnp.sum(h * h, axis=1, keepdims=True)
    lane = lax.broadcasted_iota(jnp.int32, (64, HD), 1)
    row = lax.broadcasted_iota(jnp.int32, (64, HD), 0)
    sq[...] = jnp.sum(jnp.where(lane == row, squares, 0.0), axis=0, keepdims=True)
    loads[2].wait()
    for c in range(5):
        prod = jnp.dot(scaled, w_v[:, 256 * c : 256 * c + 256], preferred_element_type=F32).astype(BF16)
        for half in range(2):
            part[:, 2 * c + half] = prod[:, HD * half : HD * half + HD].reshape(NX, 16, HD)

    @pl.when(worker & late)
    def _():
        pl.semaphore_wait(barrier, 4)

        @pl.loop(0, 8, unroll=True)
        def _(i):
            tell(hello, {"ctx": column(y_peer(i)), "grp": 0})

    @pl.when(helper & late)
    def _():
        pl.semaphore_wait(barrier, 5)
        tell(hello, {"kvh": lead, "grp": 0})

    @pl.loop(0, 3, unroll=True)
    def _(i):
        to = x_peer(i)
        send(part.at[to // NY], part_in.at[core, i], 0, {"ctx": to, "kvh": lead})

    @pl.when(helper)
    def _():
        send(part.at[x], part_in.at[core, 3], 1, {"kvh": lead})

    @pl.when(worker)
    def _():
        @pl.loop(0, 3, unroll=True)
        def _(i):
            send(sq, sq_in.at[i], 8, {"ctx": x_peer(i)})

    @pl.when(late & helper)
    def _():
        @pl.loop(0, 32, unroll=True)
        def _(i):
            to_x, to_y = plane_peer(i)
            send(part.at[to_x, to_y], direct_in.at[core, ctx], 6, {"ctx": to_x * NY + to_y, "kvh": lead, "grp": 0})

    loads[3].wait()
    for j in range(8):
        head_bias[1, j : j + 1] = bias_v[:, HD * j : HD * j + HD].astype(F32)
    head_bias[1, 8:16] = head_bias[1, 0:8]
    head_bias[1, 16:24] = jnp.broadcast_to(bias_v[:, 8 * HD : 9 * HD].astype(F32), (8, HD))
    head_bias[1, 24:32] = jnp.broadcast_to(bias_v[:, 9 * HD :].astype(F32), (8, HD))

    @pl.when(helper)
    def _():
        own = {"kvh": lead}
        send(head_bias.at[1], head_bias.at[0], 2, own)

        @pl.when(late)
        def _():
            send(kv_any, kv_v.at[0, 3], 3, own)

    @pl.when(first)
    def _():
        @pl.loop(0, 3, unroll=True)
        def _(i):
            send(kv_any, kv_v.at[core, i], 4, {"ctx": x_peer(i), "kvh": lead})

    @pl.when(helper)
    def _():
        own = {"kvh": lead}

        @pl.when(first)
        def _():
            send(kv_any, kv_v.at[0, 3], 3, own)

        send(wo_any, wo_v.at[0], 5, own)

    @pl.when(worker)
    def _():

        @pl.when(late)
        def _():
            @pl.loop(0, 32, unroll=True)
            def _(i):
                to_x, to_y = plane_peer(i)
                to = {"ctx": to_x * NY + to_y, "grp": 0}
                send(sq, direct_sq_in.at[ctx], 7, to)
                send(part.at[to_x, to_y], direct_in.at[core, ctx], 6, to)

        rows[...] = jnp.zeros_like(rows)
        wait_bytes(sq_in, recv_sem.at[8])
        sq2[...] = total([sq_in[i] for i in range(3)]) + sq[...]
        wait_bytes(part_in.at[0, 3], recv_sem.at[1])
        wait_bytes(part_in.at[:, pl.ds(0, 3)], recv_sem.at[0])
        lines = [
            total([part_in[0, i].astype(F32) for i in range(4)]),
            total([part_in[1, i].astype(F32) for i in range(3)]) + part[x].astype(F32),
        ]

        @pl.when(first)
        def _():
            for head, line in enumerate(lines):
                mid[:, head] = line[0:8].astype(BF16)

            @pl.loop(0, 7, unroll=True)
            def _(i):
                to_y = y_peer(i)
                send(mid.at[to_y], mid_in.at[i], 9, {"ctx": column(to_y)})
                send(sq2, sq2_in.at[i], 10, {"ctx": column(to_y)})

        for head, line in enumerate(lines):
            rows[head, 0:144] = line[0:9].reshape(144, HD)
            rows[head, 192:208] = line[9]
            for b in range(8):
                pieces = [rows[head, pl.ds(b + at, 8, stride=step)] for at, step in ((0, 16), (8, 16), (128, 8), (192, 8))]
                pairs[b, head] = jnp.concatenate(pieces, axis=0).astype(BF16)

        @pl.when(first)
        def _():
            pl.semaphore_wait(hello, 9)
            tell(go, {"grp": 1})

            @pl.loop(0, 8, unroll=True)
            def _(i):
                to_y = y_peer(i)
                to = {"ctx": column(to_y), "grp": 1}
                send(pairs.at[to_y], pairs_in.at[7 + i], 11, to)
                send(sq2, sq2_in.at[7 + i], 10, to)

            @pl.loop(0, 3, unroll=True)
            def _(i):
                tell(ready, {"kvh": z_peer(i) + 1})

            lane = lax.broadcasted_iota(jnp.int32, (16, HD), 1)
            row = lax.broadcasted_iota(jnp.int32, (16, HD), 0)
            wait_bytes(sq2_in.at[pl.ds(0, 7)], recv_sem.at[10])
            wait_bytes(mid_in, recv_sem.at[9])
            wait_bytes(head_bias.at[0], recv_sem.at[2])
            squares = total([sq2_in[i] for i in range(7)]) + sq2[...]
            sums = [total([mid_in[i, head].astype(F32) for i in range(7)]) + mid[y, head].astype(F32) for head in range(2)]
            pl.semaphore_wait(ready, 3)
            tell(last, {"grp": 1})
            wait_bytes(direct_sq_in, recv_sem.at[7])
            squares = total([direct_sq_in[i] for i in range(32)]) + squares
            squares = jnp.sum(jnp.where(lane == row + 16 * x, squares, 0.0), axis=1, keepdims=True)
            inverse = lax.rsqrt(squares / 8192.0 + NORM_EPS)
            wait_bytes(direct_in, recv_sem.at[6])
            for head in range(2):
                summed = total([direct_in[head, i].astype(F32) for i in range(32)]) + sums[head]
                query[y, head] = (summed * inverse + head_bias[head, pl.ds(y, 1)]).astype(BF16)

            @pl.loop(0, 7, unroll=True)
            def _(i):
                send(query.at[y], query.at[y], 12, {"ctx": column(y_peer(i))})

        @pl.when(late)
        def _():
            pl.semaphore_wait(go, 1)

            @pl.loop(0, 7, unroll=True)
            def _(i):
                to_y = y_peer(i)
                send(pairs.at[to_y], pairs_in.at[i], 11, {"ctx": column(to_y)})
                send(sq2, sq2_in.at[i], 10, {"ctx": column(to_y)})

        loads[4].wait()
        loads[6].wait()

        def scores_of(q, keys):
            return lax.dot_general(q, keys, (((1,), (1,)), ((), ())), preferred_element_type=F32) * factor

        @pl.when(first)
        def _():
            lane = lax.broadcasted_iota(jnp.int32, (HD, HD), 1)
            row = lax.broadcasted_iota(jnp.int32, (HD, HD), 0)
            wait_bytes(kv_v.at[:, pl.ds(0, 3)], recv_sem.at[4])
            wait_bytes(kv_v.at[0, 3], recv_sem.at[3])
            wait_bytes(query.at[pl.ds(0, 7)], recv_sem.at[12])
            for head in range(2):
                q = query[:, head].reshape(HD, HD)
                scores = [scores_of(q, kv_v[head, i, 0]) for i in range(NX)]
                best = functools.reduce(jnp.maximum, [jnp.max(s, axis=1, keepdims=True) for s in scores])
                weights = [jnp.exp(s - best).astype(BF16) for s in scores]
                weight_sum = total([jnp.sum(w.astype(F32), axis=1, keepdims=True) for w in weights])
                out = total([jnp.dot(w, kv_v[head, i, 1], preferred_element_type=F32) for i, w in enumerate(weights)])
                o_out[:, head] = (out / weight_sum).astype(BF16).reshape(8, 16, HD)
                lse = best + jnp.log(weight_sum)
                lse_out[head] = jnp.sum(jnp.where(lane == row, lse, 0.0), axis=0, keepdims=True)

            @pl.loop(0, 15, unroll=True)
            def _(i):
                to_y, to_grp = y_peer(i // 2), 1 - lax.rem(i, 2)
                to = {"ctx": column(to_y), "grp": to_grp}
                send(o_out.at[to_y], o_in.at[y], 13, to)
                send(lse_out, lse_in.at[y], 14, to)

            o_in[y] = o_out[y]
            lse_in[y] = lse_out[...]

        @pl.when(late)
        def _():
            lane = lax.broadcasted_iota(jnp.int32, (32, HD), 1)
            row = lax.broadcasted_iota(jnp.int32, (32, HD), 0)
            step = jnp.where(row < 16, row // 8, lax.rem(row, 2))
            wait_bytes(head_bias.at[0], recv_sem.at[2])
            wait_bytes(kv_v.at[0, 3], recv_sem.at[3])
            wait_bytes(sq2_in, recv_sem.at[10])
            squares = total([sq2_in[i] for i in range(15)]) + sq2[...]
            squares = jnp.sum(jnp.where(lane == 16 * x + 8 * step + y, squares, 0.0), axis=1, keepdims=True)
            inverse = lax.rsqrt(squares / 8192.0 + NORM_EPS)
            wait_bytes(pairs_in, recv_sem.at[11])
            for head in range(2):
                summed = total([pairs_in[i, head].astype(F32) for i in range(15)]) + pairs[y, head].astype(F32)
                summed = (summed * inverse + head_bias[head]).astype(BF16)
                q = summed[0:16]
                fresh = summed[16:32]
                cached = scores_of(q, kv_v[head, 3, 0])
                slot = lax.broadcasted_iota(jnp.int32, cached.shape, 1)
                cached = jnp.where(slot < len_ref[0], cached, FLOOR_SCORE)
                new = scores_of(q, fresh)
                key_step = lax.broadcasted_iota(jnp.int32, new.shape, 1)
                q_step = lax.broadcasted_iota(jnp.int32, new.shape, 0) // 8
                new = jnp.where(key_step <= q_step, new, FLOOR_SCORE)
                best = jnp.maximum(jnp.max(cached, axis=1, keepdims=True), jnp.max(new, axis=1, keepdims=True))
                cached = jnp.exp(cached - best).astype(BF16)
                new = jnp.exp(new - best).astype(BF16)
                weight_sum = jnp.sum(cached.astype(F32), axis=1, keepdims=True) + jnp.sum(
                    new.astype(F32), axis=1, keepdims=True
                )
                out = jnp.dot(cached, kv_v[head, 3, 1], preferred_element_type=F32)
                values = jnp.concatenate([summed[24:32].astype(F32), jnp.zeros((8, HD), F32)], axis=0).astype(BF16)
                out = out + jnp.dot(new, values, preferred_element_type=F32)
                out = out / weight_sum
                lse = jnp.broadcast_to(best + jnp.log(weight_sum), (16, HD))
                for t in range(2):
                    suf_out[pl.ds(4 * head + t, 8, stride=8)] = out[8 * t : 8 * t + 8]
                    suf_out[pl.ds(4 * head + 2 + t, 8, stride=8)] = lse[8 * t : 8 * t + 8]

            mine = pl.ds(pl.multiple_of(8 * y, 8), 8)

            @pl.loop(0, 15, unroll=True)
            def _(i):
                to_y, to_grp = y_peer(i // 2), lax.rem(i, 2)
                to = {"ctx": column(to_y), "grp": to_grp}
                send(suf_out.at[pl.ds(pl.multiple_of(8 * to_y, 8), 8)], suf_in.at[mine], 15, to)

            suf_in[mine] = suf_out[mine]

        @pl.when(first)
        def _():
            wait_bytes(lse_in.at[pl.ds(0, 7)], recv_sem.at[14])
            wait_bytes(suf_in, recv_sem.at[15])
            wait_bytes(o_in.at[pl.ds(0, 7)], recv_sem.at[13])

        @pl.when(late)
        def _():
            wait_bytes(lse_in, recv_sem.at[14])
            wait_bytes(suf_in.at[pl.ds(0, 56)], recv_sem.at[15])
            wait_bytes(o_in, recv_sem.at[13])

        lane = lax.broadcasted_iota(jnp.int32, (16, HD), 1)
        row = lax.broadcasted_iota(jnp.int32, (16, HD), 0)
        mine = lane == row + 16 * y
        own = y * NX + x
        for head in range(2):
            lses = [jnp.sum(jnp.where(mine, lse_in[i, head], 0.0), axis=1, keepdims=True) for i in range(8)]
            lses.append(jnp.concatenate([suf_in[pl.ds(4 * head + 2 + t, 8, stride=8)] for t in range(2)], axis=0)[:, 0:1])
            best = functools.reduce(jnp.maximum, lses)
            shares = [jnp.exp(v - best) for v in lses]
            outs = [o_in[i, head].astype(F32) for i in range(8)]
            outs.append(jnp.concatenate([suf_in[pl.ds(4 * head + t, 8, stride=8)] for t in range(2)], axis=0))
            att[own, head] = (total([o * s for o, s in zip(outs, shares)]) / total(shares)).astype(BF16)

        @pl.loop(0, 31, unroll=True)
        def _(i):
            to_x, to_y = plane_peer(i)
            send(att.at[own], att.at[own], 16, {"ctx": to_x * NY + to_y})

        loads[5].wait()
        wait_bytes(wo_v.at[0], recv_sem.at[5])

        @pl.when(late)
        def _():
            pl.semaphore_wait(last, 1)

        wait_bytes(att.at[pl.ds(0, 31)], recv_sem.at[16])
        projected = total(
            [
                jnp.dot(
                    jnp.concatenate([att[4 * j : 4 * j + 4, head].reshape(64, HD) for head in range(2)], axis=1),
                    jnp.concatenate([wo_v[head, HD * j : HD * j + HD] for head in range(2)], axis=0),
                    preferred_element_type=F32,
                )
                for j in range(8)
            ]
        )
        ordered = [projected[16 * b + 8 * t : 16 * b + 8 * t + 8] for t in range(2) for b in range(NX)]
        res[z] = jnp.concatenate(ordered, axis=0).astype(BF16)

        @pl.loop(0, 3, unroll=True)
        def _(i):
            send(res.at[z], res.at[z], 17, {"kvh": z_peer(i)})
            send(res.at[z], res.at[z], 17, {"kvh": z_peer(i) + 1})

        send(res.at[z], res.at[z], 17, {"kvh": lead - 1})

    wait_bytes(part_in.at[0, pl.ds(0, 3)], send_sem.at[0])

    @pl.when(first)
    def _():
        wait_bytes(kv_v.at[0, pl.ds(0, 3)], send_sem.at[4])

    @pl.when(late)
    def _():
        wait_bytes(direct_in.at[0], send_sem.at[6])

    @pl.when(helper)
    def _():
        wait_bytes(part_in.at[0, 3], send_sem.at[1])
        wait_bytes(head_bias.at[0], send_sem.at[2])
        wait_bytes(kv_v.at[0, 3], send_sem.at[3])
        wait_bytes(wo_v.at[0], send_sem.at[5])

    @pl.when(worker)
    def _():
        wait_bytes(sq_in, send_sem.at[8])

        @pl.when(first)
        def _():
            wait_bytes(mid_in, send_sem.at[9])
            wait_bytes(sq2_in, send_sem.at[10])
            wait_bytes(pairs_in.at[pl.ds(0, 8)], send_sem.at[11])
            wait_bytes(query.at[pl.ds(0, 7)], send_sem.at[12])
            wait_bytes(o_in, send_sem.at[13])
            wait_bytes(o_in.at[pl.ds(0, 7)], send_sem.at[13])
            wait_bytes(lse_in, send_sem.at[14])
            wait_bytes(lse_in.at[pl.ds(0, 7)], send_sem.at[14])

        @pl.when(late)
        def _():
            wait_bytes(direct_sq_in, send_sem.at[7])
            wait_bytes(sq2_in.at[pl.ds(0, 7)], send_sem.at[10])
            wait_bytes(pairs_in.at[pl.ds(0, 7)], send_sem.at[11])
            wait_bytes(suf_in, send_sem.at[15])
            wait_bytes(suf_in.at[pl.ds(0, 56)], send_sem.at[15])

        wait_bytes(att.at[pl.ds(0, 31)], send_sem.at[16])
        wait_bytes(res, send_sem.at[17])
        wait_bytes(res.at[pl.ds(0, 3)], send_sem.at[17])
        wait_bytes(res.at[pl.ds(0, 3)], recv_sem.at[17])

    @pl.when(helper)
    def _():
        wait_bytes(res, recv_sem.at[17])

    out_ref[...] = total([res[k].astype(F32) for k in range(4)]).astype(BF16).reshape(2, 32, HD)


def local(hidden_in, norm_gain, w_qkv, qkv_bias, kv_pool, suffix_lengths, w_out):
    anywhere = pl.BlockSpec(memory_space=pl.ANY)
    vmem = pltpu.VMEM
    return pl.pallas_call(
        kernel,
        out_shape=jax.ShapeDtypeStruct((2, 32, HD), BF16),
        in_specs=[anywhere] * 7,
        out_specs=pl.BlockSpec(memory_space=vmem),
        scratch_shapes=[
            vmem((2, 32, HD), BF16), vmem((HD,), BF16), vmem((HD, 1280), BF16), vmem((1, 1280), BF16),
            vmem((2, 4, 2, 512, HD), BF16), vmem((2, 1024, HD), BF16), pltpu.SMEM((1,), jnp.int32), vmem((2, 32, HD), F32), vmem((2, 256, HD), F32),
            vmem((4, 10, 16, HD), BF16), vmem((2, 4, 10, 16, HD), BF16), vmem((1, HD), F32), vmem((3, 1, HD), F32),
            vmem((2, 32, 16, HD), BF16), vmem((32, 1, HD), F32),
            vmem((8, 2, 16, HD), BF16), vmem((7, 2, 16, HD), BF16),
            vmem((8, 2, 32, HD), BF16), vmem((15, 2, 32, HD), BF16), vmem((1, HD), F32), vmem((15, 1, HD), F32),
            vmem((8, 2, 16, HD), BF16), vmem((8, 2, 16, HD), BF16), vmem((8, 2, 16, HD), BF16),
            vmem((2, 1, HD), F32), vmem((8, 2, 1, HD), F32), vmem((64, HD), F32), vmem((64, HD), F32),
            vmem((32, 2, 16, HD), BF16), vmem((4, 64, HD), BF16),
            pltpu.SemaphoreType.DMA((7,)), pltpu.SemaphoreType.DMA((18,)), pltpu.SemaphoreType.DMA((18,)),
            pltpu.SemaphoreType.REGULAR((5,)),
        ],
        compiler_params=pltpu.CompilerParams(
            collective_id=0, has_side_effects=True, vmem_limit_bytes=60 << 20
        ),
        name="attention_block",
    )(
        hidden_in, norm_gain, w_qkv.reshape(HD, 1280), qkv_bias, kv_pool.reshape(2, 512, HD),
        suffix_lengths, w_out,
    )


def solution(mesh):
    placed = (
        P(None, None, ("ctx", "grp")),
        P(("ctx", "grp")),
        P(("ctx", "grp"), "kvh", None),
        P("kvh", None),
        P("grp", None, "kvh", "ctx", None),
        P("ctx"),
        P("kvh", ("ctx", "grp")),
    )
    return jax.shard_map(
        local, mesh=mesh, in_specs=placed, out_specs=P(None, None, ("ctx", "grp")), check_vma=False
    )
```

```python
import functools
import math

import jax
import jax.numpy as jnp
from jax import lax
from jax.experimental import pallas as pl
from jax.experimental.pallas import tpu as pltpu
from jax.sharding import PartitionSpec as P

NORM_EPS = 1e-06
FLOOR_SCORE = -1e30
MESH = pl.DeviceIdType.MESH
NX, NY = 4, 8
HD = 128
F32, BF16 = jnp.float32, jnp.bfloat16


def zigzag(k, middle):
    if isinstance(k, int):
        return middle + (1 - 2 * (k % 2)) * ((k + 1) // 2)
    return middle + (1 - 2 * lax.rem(k, 2)) * ((k + 1) // 2)


def wait_bytes(buffer, sem):
    pltpu.make_async_copy(buffer, buffer, sem).wait()


def total(parts):
    return functools.reduce(jnp.add, parts)


def kernel(
    h_any, gain_any, w_any, bias_any, kv_any, len_any, wo_any, out_ref,
    h_v, gain_v, w_v, bias_v, kv_v, wo_v, len_ref, head_bias, rows,
    part, part_in, sq, sq_in, direct_in, direct_sq_in,
    mid, mid_in, pairs, pairs_in, sq2, sq2_in,
    query, o_out, o_in, lse_out, lse_in, suf_out, suf_in, att, res,
    local_sem, send_sem, recv_sem, flag,
):
    ctx, kvh, grp = lax.axis_index("ctx"), lax.axis_index("kvh"), lax.axis_index("grp")
    x, y = ctx // NY, lax.rem(ctx, NY)
    z, core = kvh // 2, lax.rem(kvh, 2)
    lead = kvh - core + 1
    factor = 1.0 / math.sqrt(HD)
    first, late = grp == 0, grp == 1
    helper, worker = core == 0, core == 1

    def send(src, dst, phase, target):
        pltpu.make_async_remote_copy(
            src_ref=src, dst_ref=dst, send_sem=send_sem.at[phase], recv_sem=recv_sem.at[phase],
            device_id=target, device_id_type=MESH,
        ).start()

    loads = [
        pltpu.make_async_copy(src, dst, local_sem.at[i])
        for i, (src, dst) in enumerate(
            ((h_any, h_v), (gain_any, gain_v), (w_any, w_v), (bias_any, bias_v), (kv_any, kv_v.at[1, 3]), (wo_any, wo_v.at[1]), (len_any, len_ref))
        )
    ]
    for load in loads[:4]:
        load.start()

    def x_peer(i):
        return lax.rem(x + zigzag(i, 2), NX) * NY + y

    def y_peer(i):
        return lax.rem(y + zigzag(i, 4), NY)

    def column(to_y):
        return x * NY + to_y

    def plane_peer(i):
        return lax.rem(x + zigzag(lax.rem(i, 4), 2), NX), lax.rem(y + zigzag(i // 4, 4), NY)

    def z_peer(i):
        return lax.rem(z + 1 + i, 4) * 2

    barrier = pltpu.get_barrier_semaphore()

    def tell(sem, device):
        pl.semaphore_signal(sem, inc=1, device_id=device, device_id_type=MESH)

    hello, plane, go, ready, last = (flag.at[i] for i in range(5))

    @pl.when(worker)
    def _():
        @pl.loop(0, 3, unroll=True)
        def _(i):
            tell(barrier, {"ctx": x_peer(i)})

        @pl.loop(0, 4, unroll=True)
        def _(i):
            tell(barrier, {"ctx": x_peer(i), "kvh": lead - 1})

    @pl.when(worker & first)
    def _():
        @pl.loop(0, 7, unroll=True)
        def _(i):
            tell(barrier, {"ctx": column(y_peer(i))})

        @pl.loop(0, 3, unroll=True)
        def _(i):
            tell(barrier, {"kvh": z_peer(i) + 1})

    @pl.when(worker)
    def _():
        loads[4].start()
        loads[5].start()
        loads[6].start()

    @pl.when(worker & first)
    def _():
        pl.semaphore_wait(barrier, 13)

        @pl.loop(0, 7, unroll=True)
        def _(i):
            tell(plane, {"ctx": column(y_peer(i))})

        pl.semaphore_wait(plane, 7)
        tell(barrier, {"grp": 1})
        tell(barrier, {"grp": 1, "kvh": lead - 1})

    @pl.when(helper & first)
    def _():
        pl.semaphore_wait(barrier, 4)

    loads[0].wait()
    loads[1].wait()
    h = h_v[...].astype(F32)
    h = jnp.concatenate([h[t, 8 * b : 8 * b + 8] for b in range(NX) for t in range(2)], axis=0)
    gain = gain_v[...].astype(F32).reshape(1, HD)
    scaled = (h * gain).astype(BF16)
    squares = jnp.sum(h * h, axis=1, keepdims=True)
    lane = lax.broadcasted_iota(jnp.int32, (64, HD), 1)
    row = lax.broadcasted_iota(jnp.int32, (64, HD), 0)
    sq[...] = jnp.sum(jnp.where(lane == row, squares, 0.0), axis=0, keepdims=True)
    loads[2].wait()
    for c in range(5):
        prod = jnp.dot(scaled, w_v[:, 256 * c : 256 * c + 256], preferred_element_type=F32).astype(BF16)
        for half in range(2):
            part[:, 2 * c + half] = prod[:, HD * half : HD * half + HD].reshape(NX, 16, HD)

    @pl.when(worker & late)
    def _():
        pl.semaphore_wait(barrier, 4)

        @pl.loop(0, 8, unroll=True)
        def _(i):
            tell(hello, {"ctx": column(y_peer(i)), "grp": 0})

    @pl.when(helper & late)
    def _():
        pl.semaphore_wait(barrier, 5)
        tell(hello, {"kvh": lead, "grp": 0})

    @pl.loop(0, 3, unroll=True)
    def _(i):
        to = x_peer(i)
        for c in range(0, 10, 2):
            send(part.at[to // NY, pl.ds(c, 2)], part_in.at[core, i, pl.ds(c, 2)], 0, {"ctx": to, "kvh": lead})

    @pl.when(helper)
    def _():
        send(part.at[x], part_in.at[core, 3], 1, {"kvh": lead})

    @pl.when(worker)
    def _():
        @pl.loop(0, 3, unroll=True)
        def _(i):
            send(sq, sq_in.at[i], 8, {"ctx": x_peer(i)})

    @pl.when(late)
    def _():
        @pl.loop(0, 32, unroll=True)
        def _(i):
            to_x, to_y = plane_peer(i)
            send(part.at[to_x, to_y], direct_in.at[core, ctx], 6, {"ctx": to_x * NY + to_y, "kvh": lead, "grp": 0})

    @pl.when(late & worker)
    def _():
        @pl.loop(0, 32, unroll=True)
        def _(i):
            to_x, to_y = plane_peer(i)
            send(sq, direct_sq_in.at[ctx], 7, {"ctx": to_x * NY + to_y, "grp": 0})

    loads[3].wait()
    for j in range(8):
        head_bias[1, j : j + 1] = bias_v[:, HD * j : HD * j + HD].astype(F32)
    head_bias[1, 8:16] = head_bias[1, 0:8]
    head_bias[1, 16:24] = jnp.broadcast_to(bias_v[:, 8 * HD : 9 * HD].astype(F32), (8, HD))
    head_bias[1, 24:32] = jnp.broadcast_to(bias_v[:, 9 * HD :].astype(F32), (8, HD))

    @pl.when(helper)
    def _():
        own = {"kvh": lead}
        send(head_bias.at[1], head_bias.at[0], 2, own)

        @pl.when(late)
        def _():
            send(kv_any, kv_v.at[0, 3], 3, own)

    @pl.when(first)
    def _():
        @pl.loop(0, 3, unroll=True)
        def _(i):
            send(kv_any, kv_v.at[core, i], 4, {"ctx": x_peer(i), "kvh": lead})

    @pl.when(helper)
    def _():
        own = {"kvh": lead}

        @pl.when(first)
        def _():
            send(kv_any, kv_v.at[0, 3], 3, own)

        send(wo_any, wo_v.at[0], 5, own)

    @pl.when(worker)
    def _():
        rows[...] = jnp.zeros_like(rows)
        wait_bytes(sq_in, recv_sem.at[8])
        sq2[...] = total([sq_in[i] for i in range(3)]) + sq[...]
        wait_bytes(part_in.at[0, 3], recv_sem.at[1])
        wait_bytes(part_in.at[:, pl.ds(0, 3)], recv_sem.at[0])
        lines = [
            total([part_in[0, i].astype(F32) for i in range(4)]),
            total([part_in[1, i].astype(F32) for i in range(3)]) + part[x].astype(F32),
        ]

        @pl.when(first)
        def _():
            for head, line in enumerate(lines):
                mid[:, head] = line[0:8].astype(BF16)

            @pl.loop(0, 7, unroll=True)
            def _(i):
                to_y = y_peer(i)
                send(mid.at[to_y], mid_in.at[i], 9, {"ctx": column(to_y)})
                send(sq2, sq2_in.at[i], 10, {"ctx": column(to_y)})

        for head, line in enumerate(lines):
            rows[head, 0:144] = line[0:9].reshape(144, HD)
            rows[head, 192:208] = line[9]
            for b in range(8):
                pieces = [rows[head, pl.ds(b + at, 8, stride=step)] for at, step in ((0, 16), (8, 16), (128, 8), (192, 8))]
                pairs[b, head] = jnp.concatenate(pieces, axis=0).astype(BF16)

        @pl.when(first)
        def _():
            pl.semaphore_wait(hello, 9)
            tell(go, {"grp": 1})

            @pl.loop(0, 8, unroll=True)
            def _(i):
                to_y = y_peer(i)
                to = {"ctx": column(to_y), "grp": 1}
                send(pairs.at[to_y], pairs_in.at[7 + i], 11, to)
                send(sq2, sq2_in.at[7 + i], 10, to)

            @pl.loop(0, 3, unroll=True)
            def _(i):
                tell(ready, {"kvh": z_peer(i) + 1})

            lane = lax.broadcasted_iota(jnp.int32, (16, HD), 1)
            row = lax.broadcasted_iota(jnp.int32, (16, HD), 0)
            wait_bytes(sq2_in.at[pl.ds(0, 7)], recv_sem.at[10])
            wait_bytes(mid_in, recv_sem.at[9])
            wait_bytes(head_bias.at[0], recv_sem.at[2])
            squares = total([sq2_in[i] for i in range(7)]) + sq2[...]
            sums = [total([mid_in[i, head].astype(F32) for i in range(7)]) + mid[y, head].astype(F32) for head in range(2)]
            pl.semaphore_wait(ready, 3)
            tell(last, {"grp": 1})
            wait_bytes(direct_sq_in, recv_sem.at[7])
            squares = total([direct_sq_in[i] for i in range(32)]) + squares
            squares = jnp.sum(jnp.where(lane == row + 16 * x, squares, 0.0), axis=1, keepdims=True)
            inverse = lax.rsqrt(squares / 8192.0 + NORM_EPS)
            wait_bytes(direct_in, recv_sem.at[6])
            for head in range(2):
                summed = total([direct_in[head, i].astype(F32) for i in range(32)]) + sums[head]
                query[y, head] = (summed * inverse + head_bias[head, pl.ds(y, 1)]).astype(BF16)

            @pl.loop(0, 7, unroll=True)
            def _(i):
                send(query.at[y], query.at[y], 12, {"ctx": column(y_peer(i))})

        @pl.when(late)
        def _():
            pl.semaphore_wait(go, 1)

            @pl.loop(0, 7, unroll=True)
            def _(i):
                to_y = y_peer(i)
                send(pairs.at[to_y], pairs_in.at[i], 11, {"ctx": column(to_y)})
                send(sq2, sq2_in.at[i], 10, {"ctx": column(to_y)})

        loads[4].wait()
        loads[6].wait()

        def scores_of(q, keys):
            return lax.dot_general(q, keys, (((1,), (1,)), ((), ())), preferred_element_type=F32) * factor

        @pl.when(first)
        def _():
            lane = lax.broadcasted_iota(jnp.int32, (HD, HD), 1)
            row = lax.broadcasted_iota(jnp.int32, (HD, HD), 0)
            wait_bytes(kv_v.at[:, pl.ds(0, 3)], recv_sem.at[4])
            wait_bytes(kv_v.at[0, 3], recv_sem.at[3])
            wait_bytes(query.at[pl.ds(0, 7)], recv_sem.at[12])
            for head in range(2):
                q = query[:, head].reshape(HD, HD)
                scores = [scores_of(q, kv_v[head, i, 0]) for i in range(NX)]
                best = functools.reduce(jnp.maximum, [jnp.max(s, axis=1, keepdims=True) for s in scores])
                weights = [jnp.exp(s - best).astype(BF16) for s in scores]
                weight_sum = total([jnp.sum(w.astype(F32), axis=1, keepdims=True) for w in weights])
                out = total([jnp.dot(w, kv_v[head, i, 1], preferred_element_type=F32) for i, w in enumerate(weights)])
                o_out[:, head] = (out / weight_sum).astype(BF16).reshape(8, 16, HD)
                lse = best + jnp.log(weight_sum)
                lse_out[head] = jnp.sum(jnp.where(lane == row, lse, 0.0), axis=0, keepdims=True)

            @pl.loop(0, 15, unroll=True)
            def _(i):
                to_y, to_grp = y_peer(i // 2), 1 - lax.rem(i, 2)
                to = {"ctx": column(to_y), "grp": to_grp}
                send(o_out.at[to_y], o_in.at[y], 13, to)
                send(lse_out, lse_in.at[y], 14, to)

            o_in[y] = o_out[y]
            lse_in[y] = lse_out[...]

        @pl.when(late)
        def _():
            lane = lax.broadcasted_iota(jnp.int32, (32, HD), 1)
            row = lax.broadcasted_iota(jnp.int32, (32, HD), 0)
            step = jnp.where(row < 16, row // 8, lax.rem(row, 2))
            wait_bytes(head_bias.at[0], recv_sem.at[2])
            wait_bytes(kv_v.at[0, 3], recv_sem.at[3])
            wait_bytes(sq2_in, recv_sem.at[10])
            squares = total([sq2_in[i] for i in range(15)]) + sq2[...]
            squares = jnp.sum(jnp.where(lane == 16 * x + 8 * step + y, squares, 0.0), axis=1, keepdims=True)
            inverse = lax.rsqrt(squares / 8192.0 + NORM_EPS)
            wait_bytes(pairs_in, recv_sem.at[11])
            for head in range(2):
                summed = total([pairs_in[i, head].astype(F32) for i in range(15)]) + pairs[y, head].astype(F32)
                summed = (summed * inverse + head_bias[head]).astype(BF16)
                q = summed[0:16]
                fresh = summed[16:32]
                cached = scores_of(q, kv_v[head, 3, 0])
                slot = lax.broadcasted_iota(jnp.int32, cached.shape, 1)
                cached = jnp.where(slot < len_ref[0], cached, FLOOR_SCORE)
                new = scores_of(q, fresh)
                key_step = lax.broadcasted_iota(jnp.int32, new.shape, 1)
                q_step = lax.broadcasted_iota(jnp.int32, new.shape, 0) // 8
                new = jnp.where(key_step <= q_step, new, FLOOR_SCORE)
                best = jnp.maximum(jnp.max(cached, axis=1, keepdims=True), jnp.max(new, axis=1, keepdims=True))
                cached = jnp.exp(cached - best).astype(BF16)
                new = jnp.exp(new - best).astype(BF16)
                weight_sum = jnp.sum(cached.astype(F32), axis=1, keepdims=True) + jnp.sum(
                    new.astype(F32), axis=1, keepdims=True
                )
                out = jnp.dot(cached, kv_v[head, 3, 1], preferred_element_type=F32)
                values = jnp.concatenate([summed[24:32].astype(F32), jnp.zeros((8, HD), F32)], axis=0).astype(BF16)
                out = out + jnp.dot(new, values, preferred_element_type=F32)
                out = out / weight_sum
                lse = jnp.broadcast_to(best + jnp.log(weight_sum), (16, HD))
                for t in range(2):
                    suf_out[pl.ds(4 * head + t, 8, stride=8)] = out[8 * t : 8 * t + 8]
                    suf_out[pl.ds(4 * head + 2 + t, 8, stride=8)] = lse[8 * t : 8 * t + 8]

            mine = pl.ds(pl.multiple_of(8 * y, 8), 8)

            @pl.loop(0, 15, unroll=True)
            def _(i):
                to_y, to_grp = y_peer(i // 2), lax.rem(i, 2)
                to = {"ctx": column(to_y), "grp": to_grp}
                send(suf_out.at[pl.ds(pl.multiple_of(8 * to_y, 8), 8)], suf_in.at[mine], 15, to)

            suf_in[mine] = suf_out[mine]

        @pl.when(first)
        def _():
            wait_bytes(lse_in.at[pl.ds(0, 7)], recv_sem.at[14])
            wait_bytes(suf_in, recv_sem.at[15])
            wait_bytes(o_in.at[pl.ds(0, 7)], recv_sem.at[13])

        @pl.when(late)
        def _():
            wait_bytes(lse_in, recv_sem.at[14])
            wait_bytes(suf_in.at[pl.ds(0, 56)], recv_sem.at[15])
            wait_bytes(o_in, recv_sem.at[13])

        lane = lax.broadcasted_iota(jnp.int32, (16, HD), 1)
        row = lax.broadcasted_iota(jnp.int32, (16, HD), 0)
        mine = lane == row + 16 * y
        own = y * NX + x
        for head in range(2):
            lses = [jnp.sum(jnp.where(mine, lse_in[i, head], 0.0), axis=1, keepdims=True) for i in range(8)]
            lses.append(jnp.concatenate([suf_in[pl.ds(4 * head + 2 + t, 8, stride=8)] for t in range(2)], axis=0)[:, 0:1])
            best = functools.reduce(jnp.maximum, lses)
            shares = [jnp.exp(v - best) for v in lses]
            outs = [o_in[i, head].astype(F32) for i in range(8)]
            outs.append(jnp.concatenate([suf_in[pl.ds(4 * head + t, 8, stride=8)] for t in range(2)], axis=0))
            att[own, head] = (total([o * s for o, s in zip(outs, shares)]) / total(shares)).astype(BF16)

        @pl.loop(0, 31, unroll=True)
        def _(i):
            to_x, to_y = plane_peer(i)
            send(att.at[own], att.at[own], 16, {"ctx": to_x * NY + to_y})

        loads[5].wait()
        wait_bytes(wo_v.at[0], recv_sem.at[5])

        @pl.when(late)
        def _():
            pl.semaphore_wait(last, 1)

        wait_bytes(att.at[pl.ds(0, 31)], recv_sem.at[16])
        projected = total(
            [
                jnp.dot(
                    jnp.concatenate([att[4 * j : 4 * j + 4, head].reshape(64, HD) for head in range(2)], axis=1),
                    jnp.concatenate([wo_v[head, HD * j : HD * j + HD] for head in range(2)], axis=0),
                    preferred_element_type=F32,
                )
                for j in range(8)
            ]
        )
        ordered = [projected[16 * b + 8 * t : 16 * b + 8 * t + 8] for t in range(2) for b in range(NX)]
        res[z] = jnp.concatenate(ordered, axis=0).astype(BF16)

        @pl.loop(0, 3, unroll=True)
        def _(i):
            send(res.at[z], res.at[z], 17, {"kvh": z_peer(i)})
            send(res.at[z], res.at[z], 17, {"kvh": z_peer(i) + 1})

        send(res.at[z], res.at[z], 17, {"kvh": lead - 1})

    wait_bytes(part_in.at[0, pl.ds(0, 3)], send_sem.at[0])

    @pl.when(first)
    def _():
        wait_bytes(kv_v.at[0, pl.ds(0, 3)], send_sem.at[4])

    @pl.when(late)
    def _():
        wait_bytes(direct_in.at[0], send_sem.at[6])

    @pl.when(helper)
    def _():
        wait_bytes(part_in.at[0, 3], send_sem.at[1])
        wait_bytes(head_bias.at[0], send_sem.at[2])
        wait_bytes(kv_v.at[0, 3], send_sem.at[3])
        wait_bytes(wo_v.at[0], send_sem.at[5])

    @pl.when(worker)
    def _():
        wait_bytes(sq_in, send_sem.at[8])

        @pl.when(first)
        def _():
            wait_bytes(mid_in, send_sem.at[9])
            wait_bytes(sq2_in, send_sem.at[10])
            wait_bytes(pairs_in.at[pl.ds(0, 8)], send_sem.at[11])
            wait_bytes(query.at[pl.ds(0, 7)], send_sem.at[12])
            wait_bytes(o_in, send_sem.at[13])
            wait_bytes(o_in.at[pl.ds(0, 7)], send_sem.at[13])
            wait_bytes(lse_in, send_sem.at[14])
            wait_bytes(lse_in.at[pl.ds(0, 7)], send_sem.at[14])

        @pl.when(late)
        def _():
            wait_bytes(direct_sq_in, send_sem.at[7])
            wait_bytes(sq2_in.at[pl.ds(0, 7)], send_sem.at[10])
            wait_bytes(pairs_in.at[pl.ds(0, 7)], send_sem.at[11])
            wait_bytes(suf_in, send_sem.at[15])
            wait_bytes(suf_in.at[pl.ds(0, 56)], send_sem.at[15])

        wait_bytes(att.at[pl.ds(0, 31)], send_sem.at[16])
        wait_bytes(res, send_sem.at[17])
        wait_bytes(res.at[pl.ds(0, 3)], send_sem.at[17])
        wait_bytes(res.at[pl.ds(0, 3)], recv_sem.at[17])

    @pl.when(helper)
    def _():
        wait_bytes(res, recv_sem.at[17])

    out_ref[...] = total([res[k].astype(F32) for k in range(4)]).astype(BF16).reshape(2, 32, HD)


def local(hidden_in, norm_gain, w_qkv, qkv_bias, kv_pool, suffix_lengths, w_out):
    anywhere = pl.BlockSpec(memory_space=pl.ANY)
    vmem = pltpu.VMEM
    return pl.pallas_call(
        kernel,
        out_shape=jax.ShapeDtypeStruct((2, 32, HD), BF16),
        in_specs=[anywhere] * 7,
        out_specs=pl.BlockSpec(memory_space=vmem),
        scratch_shapes=[
            vmem((2, 32, HD), BF16), vmem((HD,), BF16), vmem((HD, 1280), BF16), vmem((1, 1280), BF16),
            vmem((2, 4, 2, 512, HD), BF16), vmem((2, 1024, HD), BF16), pltpu.SMEM((1,), jnp.int32), vmem((2, 32, HD), F32), vmem((2, 256, HD), F32),
            vmem((4, 10, 16, HD), BF16), vmem((2, 4, 10, 16, HD), BF16), vmem((1, HD), F32), vmem((3, 1, HD), F32),
            vmem((2, 32, 16, HD), BF16), vmem((32, 1, HD), F32),
            vmem((8, 2, 16, HD), BF16), vmem((7, 2, 16, HD), BF16),
            vmem((8, 2, 32, HD), BF16), vmem((15, 2, 32, HD), BF16), vmem((1, HD), F32), vmem((15, 1, HD), F32),
            vmem((8, 2, 16, HD), BF16), vmem((8, 2, 16, HD), BF16), vmem((8, 2, 16, HD), BF16),
            vmem((2, 1, HD), F32), vmem((8, 2, 1, HD), F32), vmem((64, HD), F32), vmem((64, HD), F32),
            vmem((32, 2, 16, HD), BF16), vmem((4, 64, HD), BF16),
            pltpu.SemaphoreType.DMA((7,)), pltpu.SemaphoreType.DMA((18,)), pltpu.SemaphoreType.DMA((18,)),
            pltpu.SemaphoreType.REGULAR((5,)),
        ],
        compiler_params=pltpu.CompilerParams(
            collective_id=0, has_side_effects=True, vmem_limit_bytes=60 << 20
        ),
        name="attention_block",
    )(
        hidden_in, norm_gain, w_qkv.reshape(HD, 1280), qkv_bias, kv_pool.reshape(2, 512, HD),
        suffix_lengths, w_out,
    )


def solution(mesh):
    placed = (
        P(None, None, ("ctx", "grp")),
        P(("ctx", "grp")),
        P(("ctx", "grp"), "kvh", None),
        P("kvh", None),
        P("grp", None, "kvh", "ctx", None),
        P("ctx"),
        P("kvh", ("ctx", "grp")),
    )
    return jax.shard_map(
        local, mesh=mesh, in_specs=placed, out_specs=P(None, None, ("ctx", "grp")), check_vma=False
    )
```
